128 devices in a mesh: slab: 4 (over y_hi, core), col: 32 (over z, x, y_lo).
Axes of the slice: x: 4, y: 4 (y_hi: 2, y_lo: 2; y = y_hi * 2 + y_lo), z: 4, core: 2. Of those that a mesh axis runs over, the one named last changes fastest.
Arguments:
- offsets: float32 [16, 64, 3, 8192], P('slab', 'col'), may hold values from 0 to 1
- charges: float32 [16, 64, 8192], P('slab', 'col'), may hold values from -0.6 to 0.6
- check_to_equiv: float32 [98, 98], replicated, may hold values from -0.625 to 0.625
- m2m_matrix: float32 [98, 784], replicated, may hold values from -0.21875 to 0.21875
- m2l_matrix: float32 [98, 30968], replicated, may hold values from -0.046875 to 0.046875
Outputs:
- near_field: float32 [16, 64, 4, 512], P('slab', 'col')
- far_level2: float32 [98, 2048], P(None, ('slab', 'col'))
- far_level3: float32 [98, 256], P(None, ('slab', 'col'))
The draws below stay inside these ranges and needn't reach their ends.
All inputs are finite; a program needn't handle non-finite values.
Results may differ from the reference program's by a relative error of at most 0.00014.
Values sent between devices are 32-bit elements; how exact they have to be, the bound alone decides.
A program may use at most 192 MiB of HBM per device.

```python
import jax
import jax.numpy as jnp
from jax import lax

Q = 64
QT = 4
P_SIZE = 5
NS = 98
OFFS = 316
GX = 128
GY = 64
GZ = 16


def levels(own_key, dims, shards, low, high):
    level = 1.0
    for position, blocks in shards:
        steps = jax.random.uniform(jax.random.fold_in(jax.random.fold_in(own_key, 6), position), (blocks,), jnp.float32, low / len(shards), high / len(shards))
        level = level * jnp.repeat(jnp.exp(steps), dims[position] // blocks).reshape((-1,) + (1,) * (len(dims) - 1 - position))
    return level


def normal_values(stream_key, extent, width, reach, shards=(), held_as=jnp.bfloat16):
    values = width * jax.random.normal(stream_key, extent, jnp.float32)
    if shards:
        values = values * levels(stream_key, extent, shards, -0.22, 0.18)
    return jnp.clip(values, -reach, reach).astype(held_as)


def setup_inputs(seed: int = 0) -> dict:
    key_of = jax.random.split(jax.random.key(seed), 6)
    offsets = jnp.clip(1.0 * jax.random.uniform(key_of[0], (GZ, GY, 3, GX * Q), jnp.float32) ** levels(key_of[0], (GZ, GY, 3, GX * Q), ((0, 4), (1, 32)), -0.2, 0.2), 0.0, 1.0)
    charges = normal_values(key_of[1], (GZ, GY, GX * Q), 0.1, 0.6, ((0, 4), (1, 32)), jnp.float32)
    check_to_equiv = normal_values(key_of[2], (NS, NS), NS ** -0.5, 0.625, (), jnp.float32)
    m2m_matrix = normal_values(key_of[3], (NS, 8 * NS), (8 * NS) ** -0.5, 0.21875, (), jnp.float32)
    m2l_matrix = normal_values(key_of[4], (NS, OFFS * NS), (189 * NS) ** -0.5, 0.046875, (), jnp.float32)
    return dict(offsets=offsets, charges=charges, check_to_equiv=check_to_equiv, m2m_matrix=m2m_matrix, m2l_matrix=m2l_matrix)


SOFTEN = 0.0625
CHECK_SIDE = 1.45

def surface_table(points_side):
    picked = []
    for along_z in range(points_side):
        for along_y in range(points_side):
            for along_x in range(points_side):
                lowest = min(along_z, along_y, along_x)
                highest = max(along_z, along_y, along_x)
                if lowest == 0 or highest == points_side - 1:
                    picked.append([(float(along_z) / (points_side - 1) - 0.5) * (2.0 * CHECK_SIDE) + 0.5, (float(along_y) / (points_side - 1) - 0.5) * (2.0 * CHECK_SIDE) + 0.5, (float(along_x) / (points_side - 1) - 0.5) * (2.0 * CHECK_SIDE) + 0.5])
    return picked

def offset_table():
    listed = []
    for shift_z in range(-3, 4):
        for shift_y in range(-3, 4):
            for shift_x in range(-3, 4):
                if max(abs(shift_z), abs(shift_y), abs(shift_x)) >= 2:
                    listed.append([shift_z, shift_y, shift_x])
    return listed

def pair_terms(target_pos, source_pos, source_chg, shift_z, shift_y, shift_x, keep_mask):
    delta_z = target_pos[:, :, 0, :, :, None] - source_pos[:, :, 0, :, None, :] - shift_z
    delta_y = target_pos[:, :, 1, :, :, None] - source_pos[:, :, 1, :, None, :] - shift_y
    delta_x = target_pos[:, :, 2, :, :, None] - source_pos[:, :, 2, :, None, :] - shift_x
    inverse = lax.rsqrt(delta_z * delta_z + delta_y * delta_y + delta_x * delta_x + SOFTEN)
    weight = source_chg[:, :, :, None, :] * inverse * keep_mask
    cubed_term = weight * inverse * inverse
    return jnp.stack([lax.optimization_barrier(jnp.sum(weight, axis=-1)), lax.optimization_barrier(jnp.sum(cubed_term * delta_z, axis=-1)), lax.optimization_barrier(jnp.sum(cubed_term * delta_y, axis=-1)), lax.optimization_barrier(jnp.sum(cubed_term * delta_x, axis=-1))], axis=2)

def near_block(target_pos, padded_pos, padded_chg):
    z_cells = target_pos.shape[0]
    y_cells = target_pos.shape[1]
    x_cells = target_pos.shape[3]
    target_count = target_pos.shape[4]
    per_leaf = padded_pos.shape[-1]
    slot_shift = jnp.repeat(jnp.array([-1.0, 0.0, 1.0], jnp.float32), per_leaf)[None, :]
    target_slot = jnp.arange(target_count, dtype=jnp.int32)[:, None]
    source_slot = jnp.arange(3 * per_leaf, dtype=jnp.int32)[None, :] - per_leaf
    center_keep = jnp.where(target_slot == source_slot, 0.0, 1.0).astype(jnp.float32)
    ones_keep = jnp.ones_like(center_keep)
    summed = jnp.zeros((z_cells, y_cells, 4, x_cells, target_count), jnp.float32)
    for shift_z in (-1, 0, 1):
        for shift_y in (-1, 0, 1):
            window_pos = padded_pos[1 + shift_z:1 + shift_z + z_cells, 1 + shift_y:1 + shift_y + y_cells]
            window_chg = padded_chg[1 + shift_z:1 + shift_z + z_cells, 1 + shift_y:1 + shift_y + y_cells]
            source_pos = jnp.concatenate([window_pos[:, :, :, 1 + shift_x:1 + shift_x + x_cells, :] for shift_x in (-1, 0, 1)], axis=-1)
            source_chg = jnp.concatenate([window_chg[:, :, 1 + shift_x:1 + shift_x + x_cells, :] for shift_x in (-1, 0, 1)], axis=-1)
            keep_mask = center_keep if shift_z == 0 and shift_y == 0 else ones_keep
            summed = summed + pair_terms(target_pos, source_pos, source_chg, float(shift_z), float(shift_y), slot_shift, keep_mask)
    return summed

def check_row(row_pos, row_chg, surface):
    delta_z = surface[:, 0, None, None] - row_pos[None, 0]
    delta_y = surface[:, 1, None, None] - row_pos[None, 1]
    delta_x = surface[:, 2, None, None] - row_pos[None, 2]
    inverse = lax.rsqrt(delta_z * delta_z + delta_y * delta_y + delta_x * delta_x)
    return lax.optimization_barrier(jnp.sum(row_chg[None] * inverse, axis=-1))

def upward(density, m2m_matrix):
    points, z_cells, y_cells, x_cells = density.shape
    grouped = density.reshape(points, z_cells // 2, 2, y_cells // 2, 2, x_cells // 2, 2)
    grouped = jnp.transpose(grouped, (2, 4, 6, 0, 1, 3, 5)).reshape(8 * points, -1)
    parent = jnp.dot(m2m_matrix, grouped, precision=lax.Precision.HIGHEST, preferred_element_type=jnp.float32)
    return parent.reshape(points, z_cells // 2, y_cells // 2, x_cells // 2)

def interact(density_grid, owned, m2l_matrix, factor):
    points, z_cells, y_cells, x_cells = density_grid.shape
    shifts = jnp.asarray(offset_table(), jnp.int32)
    cell_z = (owned // (y_cells * x_cells))[None, :]
    cell_y = (owned // x_cells % y_cells)[None, :]
    cell_x = (owned % x_cells)[None, :]
    source_z = cell_z + shifts[:, 0:1]
    source_y = cell_y + shifts[:, 1:2]
    source_x = cell_x + shifts[:, 2:3]
    inside = (source_z >= 0) & (source_z < z_cells) & (source_y >= 0) & (source_y < y_cells) & (source_x >= 0) & (source_x < x_cells)
    parent_near = (jnp.abs(jnp.floor_divide(source_z, 2) - jnp.floor_divide(cell_z, 2)) <= 1) & (jnp.abs(jnp.floor_divide(source_y, 2) - jnp.floor_divide(cell_y, 2)) <= 1) & (jnp.abs(jnp.floor_divide(source_x, 2) - jnp.floor_divide(cell_x, 2)) <= 1)
    usable = (inside & parent_near).astype(jnp.float32)
    flat_index = jnp.clip(source_z, 0, z_cells - 1) * (y_cells * x_cells) + jnp.clip(source_y, 0, y_cells - 1) * x_cells + jnp.clip(source_x, 0, x_cells - 1)
    flat_density = density_grid.reshape(points, -1)
    picked = jnp.take(flat_density, flat_index.reshape(-1), axis=1).reshape(points, shifts.shape[0], -1) * usable[None]
    stacked = jnp.transpose(picked, (1, 0, 2)).reshape(shifts.shape[0] * points, -1)
    return factor * jnp.dot(m2l_matrix, stacked, precision=lax.Precision.HIGHEST, preferred_element_type=jnp.float32)

def leaf_densities(positions, charge_grid, check_to_equiv):
    z_cells, y_cells, x_cells = (charge_grid.shape[0], charge_grid.shape[1], charge_grid.shape[2])
    points = check_to_equiv.shape[0]
    surface = jnp.asarray(surface_table(P_SIZE), jnp.float32)
    row_pos = positions.reshape(z_cells * y_cells, 3, x_cells, Q)
    row_chg = charge_grid.reshape(z_cells * y_cells, x_cells, Q)

    def check_bundle(bundle):
        return check_row(bundle[0], bundle[1], surface)
    checks = lax.map(check_bundle, (row_pos, row_chg))
    checks = jnp.transpose(checks, (1, 0, 2)).reshape(points, -1)
    leaf_density = jnp.dot(check_to_equiv, checks, precision=lax.Precision.HIGHEST, preferred_element_type=jnp.float32)
    return leaf_density.reshape(points, z_cells, y_cells, x_cells)

def reference(offsets, charges, check_to_equiv, m2m_matrix, m2l_matrix):
    z_cells, y_cells, merged = charges.shape
    x_cells = merged // Q
    positions = offsets.reshape(z_cells, y_cells, 3, x_cells, Q)
    charge_grid = charges.reshape(z_cells, y_cells, x_cells, Q)
    padded_pos = jnp.pad(positions, ((1, 1), (1, 1), (0, 0), (1, 1), (0, 0)))
    padded_chg = jnp.pad(charge_grid, ((1, 1), (1, 1), (1, 1), (0, 0)))
    targets = positions[..., :QT]

    def one_plane(plane_at):
        window_pos = lax.dynamic_slice_in_dim(padded_pos, plane_at, 3, 0)
        window_chg = lax.dynamic_slice_in_dim(padded_chg, plane_at, 3, 0)
        plane_targets = lax.dynamic_slice_in_dim(targets, plane_at, 1, 0)
        return near_block(plane_targets, window_pos, window_chg)[0]
    near_terms = lax.map(one_plane, jnp.arange(z_cells, dtype=jnp.int32))
    near_field = near_terms.reshape(z_cells, y_cells, 4, x_cells * QT)
    leaf_density = leaf_densities(positions, charge_grid, check_to_equiv)
    level_one = upward(leaf_density, m2m_matrix)
    level_two = upward(level_one, m2m_matrix)
    level_three = upward(level_two, m2m_matrix)
    cells_two = level_two.shape[1] * level_two.shape[2] * level_two.shape[3]
    cells_three = level_three.shape[1] * level_three.shape[2] * level_three.shape[3]
    far_level2 = interact(level_two, jnp.arange(cells_two, dtype=jnp.int32), m2l_matrix, 1.0)
    far_level3 = interact(level_three, jnp.arange(cells_three, dtype=jnp.int32), m2l_matrix, 0.5)
    return (near_field, far_level2, far_level3)
```

```python
import jax
import jax.numpy as jnp
from jax import lax
from jax.experimental import pallas as pl
from jax.experimental.pallas import tpu as pltpu
from jax.sharding import PartitionSpec as P

Q = 64
QT = 4
P_SIZE = 5
NS = 98
W = 128
SOFTEN = 0.0625
CHECK_SIDE = 1.45
F32 = jnp.float32
BF16 = jnp.bfloat16

COORD = [(float(g) / (P_SIZE - 1) - 0.5) * (2.0 * CHECK_SIDE) + 0.5 for g in range(P_SIZE)]
SURFACE = [
    (a, b, c)
    for a in range(P_SIZE)
    for b in range(P_SIZE)
    for c in range(P_SIZE)
    if min(a, b, c) == 0 or max(a, b, c) == P_SIZE - 1
]
OFFSETS = [
    (z, y, x)
    for z in range(-3, 4)
    for y in range(-3, 4)
    for x in range(-3, 4)
    if max(abs(z), abs(y), abs(x)) >= 2
]
K_ALL = len(OFFSETS) * NS
CHUNK = 512
MAIN = K_ALL // CHUNK * CHUNK
REST = K_ALL - MAIN


def split(x):
    high = x.astype(BF16)
    return high, (x - high.astype(F32)).astype(BF16)


def dot(a, b):
    return jnp.dot(a, b, preferred_element_type=F32)


def dot_t(a, b):
    return lax.dot_general(a, b, (((1,), (1,)), ((), ())), preferred_element_type=F32)


def dot3(a, b, d=dot):
    ah, al = split(a)
    bh, bl = split(b)
    return d(ah, bh) + d(ah, bl) + d(al, bh)


def squares_and_checks(src_ref, check, zz, yy, xx):
    def one_row(row, carry):
        for comp, table in ((0, zz), (1, yy), (2, xx)):
            value = src_ref[row, comp]
            for g in range(P_SIZE):
                delta = COORD[g] - value
                table[g] = delta * delta
        charge = src_ref[row, 3]
        lanes = pl.ds(pl.multiple_of(row * W, W), W)
        pair = None
        for k, (a, b, c) in enumerate(SURFACE):
            if pair != (a, b):
                pair, plane = (a, b), zz[a] + yy[b]
            term = charge * lax.rsqrt(plane + xx[c])
            check[k : k + 1, lanes] = jnp.sum(term, axis=0, keepdims=True)
        return carry

    lax.fori_loop(0, 8, one_row, 0)


def pad_matrices(c2e_ref, m2m_ref, c2e, m2m):
    c2e[...] = jnp.zeros_like(c2e)
    m2m[...] = jnp.zeros_like(m2m)
    c2e[0:NS, 0:NS] = c2e_ref[...]
    for octant in range(8):
        m2m[0:NS, octant * W : octant * W + NS] = m2m_ref[:, octant * NS : (octant + 1) * NS]


def upward_two(check, c2e, m2m, grouped, parity):
    density = dot3(c2e[...], check[...])
    high, low = split(density)
    leaf = lax.broadcasted_iota(jnp.int32, (2 * W, W), 0)
    lane = lax.broadcasted_iota(jnp.int32, (2 * W, W), 1)
    cell = (lane // 64) * W + 4 * (lane % 32) + 2 * ((lane // 32) % 2)
    for bx in range(2):
        pick = jnp.where(leaf == cell + bx, 1.0, 0.0).astype(BF16)
        for bz in range(2):
            for by in range(2):
                one, two = (bz * 2 + by) * W, ((bz + 2) * 2 + by) * W
                octant = 4 * bz + 2 * by + bx
                for half, part in enumerate((high, low)):
                    both = jnp.concatenate([part[:, one : one + W], part[:, two : two + W]], axis=1)
                    grouped[half, octant * W : (octant + 1) * W, :] = dot(both, pick).astype(BF16)
    mh, ml = split(m2m[...])
    level_one = dot(mh, grouped[0]) + dot(mh, grouped[1]) + dot(ml, grouped[0])
    turned = jnp.transpose(level_one)
    total = jnp.zeros((32, W), F32)
    for bz in range(2):
        for bx in range(2):
            at = pl.multiple_of((4 * bz + 2 * parity + bx) * W, W)
            block = turned[(bz * 2 + bx) * 32 : (bz * 2 + bx + 1) * 32]
            total = total + dot3(block, m2m[:, pl.ds(at, W)], dot_t)
    return total


def shifted_sources(src_ref, moved):
    lane = lax.broadcasted_iota(jnp.int32, (Q, W), 1)

    def one(row, carry):
        for comp in range(4):
            value = src_ref[row, comp]
            left = pltpu.roll(value, 1, 1)
            right = pltpu.roll(value, W - 1, 1)
            if comp == 3:
                left = jnp.where(lane == 0, 0.0, left)
                right = jnp.where(lane == W - 1, 0.0, right)
            moved[0, row, comp] = left
            moved[1, row, comp] = value
            moved[2, row, comp] = right
        return carry

    lax.fori_loop(0, 8, one, 0)


def pair_rows(t_ref, moved, acc, zs, ys, sz, sy):
    tz, ty = zs + 1 - sz, ys + 1 - sy
    row = zs * 2 + ys
    centre = (sz == 0) & (sy == 0)
    sub = lax.broadcasted_iota(jnp.int32, (8, W), 0)
    rows = [jnp.broadcast_to(t_ref[tz, ty, k : k + 1, :], (8, W)) for k in range(12)]
    target_z = [rows[i] - sz.astype(F32) for i in range(QT)]
    target_y = [rows[QT + i] - sy.astype(F32) for i in range(QT)]
    sums = [jnp.zeros((8, W), F32) for _ in range(16)]
    for dx in range(3):
        target_x = [rows[2 * QT + i] - float(dx - 1) for i in range(QT)]
        for v in range(8):
            at = slice(8 * v, 8 * v + 8)
            z, y, x, q = [moved[dx, row, comp, at, :] for comp in range(4)]
            for i in range(QT):
                dz, dy, ddx = target_z[i] - z, target_y[i] - y, target_x[i] - x
                inverse = lax.rsqrt(dz * dz + dy * dy + (ddx * ddx + SOFTEN))
                weight = q * inverse
                if dx == 1 and v == 0:
                    weight = jnp.where((sub == i) & centre, 0.0, weight)
                cubed = weight * (inverse * inverse)
                sums[4 * i] += weight
                sums[4 * i + 1] += cubed * dz
                sums[4 * i + 2] += cubed * dy
                sums[4 * i + 3] += cubed * ddx
    for k in range(16):
        acc[tz, ty, k] += sums[k]


def pair_loop(t_ref, moved, acc, z_first, z_count, z_step, y_first, y_count, y_step):
    def one(p, carry):
        iz, iy = z_first + z_step * (p // y_count), y_first + y_step * (p % y_count)
        pair_rows(t_ref, moved, acc, iz // 3, iy // 3, 1 - iz % 3, 1 - iy % 3)
        return carry

    lax.fori_loop(0, z_count * y_count, one, 0)


def sum_rows(acc, sums, z, y):
    sums[z, y] = jnp.sum(acc[z, y], axis=1)


def densities_three(two, three, grouped, m2m):
    def gather(n, carry):
        z, y = n // 8, n % 8
        for bz in range(2):
            for by in range(2):
                for bx in range(2):
                    octant = 4 * bz + 2 * by + bx
                    grouped[pl.ds(pl.multiple_of(n * 16, 16), 16), octant * W : (octant + 1) * W] = two[
                        2 * z + bz, 2 * y + by, pl.ds(8 + bx, 16, stride=2), :
                    ]
        return carry

    lax.fori_loop(0, 16, gather, 0)
    level_three = dot3(grouped[...], m2m[...], dot_t)
    for n in range(16):
        three[n // 8, n % 8, 8:24, :] = level_three[n * 16 : (n + 1) * 16]


def stack_sources(two, three, stacked, slab, col):
    z2, y2, x2 = slab, col // 2, 16 * (col % 2)
    z3, y3, x3 = slab // 2, 4 * (slab % 2) + col // 8, 2 * (col % 8)
    sub = lax.broadcasted_iota(jnp.int32, (24, W), 0)
    lane = lax.broadcasted_iota(jnp.int32, (24, W), 1)

    def use(cell, shift, size):
        at = cell + shift
        near = jnp.abs(at // 2 - cell // 2) <= 1
        return (at >= 0) & (at < size) & near, jnp.clip(at, 0, size - 1)

    pending = None
    for o, (oz, oy, ox) in enumerate(OFFSETS):
        uz2, sz2 = use(z2, oz, 4)
        uy2, sy2 = use(y2, oy, 16)
        uz3, sz3 = use(z3, oz, 2)
        uy3, sy3 = use(y3, oy, 8)
        keep2 = jnp.where(uz2 & uy2, 1.0, 0.0).astype(F32)
        keep3 = jnp.where(uz3 & uy3, 1.0, 0.0).astype(F32)
        value = jnp.concatenate(
            [
                two[sz2, sy2, pl.ds(8 + x2 + ox, 16), :] * keep2,
                three[sz3, sy3, pl.ds(8 + x3 + ox, 8), :] * keep3,
            ],
            axis=0,
        )
        if ox == 3:
            value = jnp.where(sub % 2 == 0, value, 0.0)
        if ox == -3:
            value = jnp.where(sub % 2 == 1, value, 0.0)
        tile, start = divmod(o * NS, W)
        if start:
            value = pltpu.roll(value, start, 1)
        filled = value if pending is None else jnp.where(lane < start, pending, value)
        if start + NS >= W:
            stacked[:, tile * W : (tile + 1) * W] = filled
            pending = value if start + NS > W else None
        else:
            pending = filled
    if pending is not None:
        stacked[:, K_ALL // W * W : K_ALL // W * W + W] = jnp.where(lane < K_ALL % W, pending, 0.0)


def translate(stacked, matrix, tail):
    def one(n, total):
        at = pl.ds(pl.multiple_of(n * CHUNK, CHUNK), CHUNK)
        return total + dot3(stacked[:, at], matrix[:, at], dot_t)

    total = lax.fori_loop(0, MAIN // CHUNK, one, jnp.zeros((24, NS), F32))
    return total + dot3(stacked[:, MAIN : MAIN + REST], tail[...], dot_t)


def interleave(lines, out_ref):
    source = lax.broadcasted_iota(jnp.int32, (QT * W, QT * W), 0)
    place = lax.broadcasted_iota(jnp.int32, (QT * W, QT * W), 1)
    move = jnp.where(place == QT * (source % W) + source // W, 1.0, 0.0).astype(BF16)
    value = lines[...]
    high, low = split(value)
    lowest = (value - high.astype(F32) - low.astype(F32)).astype(BF16)
    result = dot(high, move) + dot(low, move) + dot(lowest, move)
    for row in range(8):
        out_ref[row // 2, row % 2] = result[4 * row : 4 * row + 4]


SIDES = [(s, c) for s in (-1, 0, 1) for c in (-1, 0, 1) if (s, c) != (0, 0)]


def border(step, size):
    return {-1: slice(0, 1), 0: slice(1, size + 1), 1: slice(size + 1, size + 2)}[step]


def edge(step, size):
    return {-1: slice(1, 2), 0: slice(1, size + 1), 1: slice(size, size + 1)}[step]


def whole_kernel(
    src_ref, c2e_ref, m2m_ref, m2l_ref, near_ref, far2_ref, far3_ref,
    targets, back, acc, sums, moved, lines, m2m, c2e, check, zz, yy, xx, grouped_up,
    part, arrived, two, three, grouped, stacked, matrix, tail,
    load_sem, t_send, t_recv, b_send, b_recv, p_sem, a_send, a_recv, x_send, x_recv, z_send, z_recv,
):
    slab, col = lax.axis_index("slab"), lax.axis_index("col")
    zc, xc, low_y = col // 8, (col // 2) % 4, col % 2
    place = slab * 2 + low_y

    def local_at(k):
        to = lax.rem(place + k, 8)
        return to // 2, (col // 2) * 2 + lax.rem(to, 2)

    def along_x(k):
        return slab, zc * 8 + lax.rem(xc + k, 4) * 2 + low_y

    def along_z(k):
        return slab, lax.rem(zc + k, 4) * 8 + xc * 2 + low_y

    def exists(s, c):
        return (slab + s >= 0) & (slab + s < 4) & (col + c >= 0) & (col + c < 32)

    main = pltpu.make_async_copy(m2l_ref.at[:, pl.ds(0, MAIN)], matrix, load_sem.at[0])
    rest = pltpu.make_async_copy(m2l_ref.at[:, pl.ds(MAIN, REST)], tail, load_sem.at[1])
    main.start()
    rest.start()
    targets[...] = jnp.zeros_like(targets)
    back[...] = jnp.zeros_like(back)
    two[:, :, 0:8, :] = jnp.zeros((4, 16, 8, W), F32)
    two[:, :, 40:48, :] = jnp.zeros((4, 16, 8, W), F32)

    barrier = pltpu.get_barrier_semaphore()
    others = [local_at(k) for k in range(1, 8)]
    others += [along_x(k) for k in range(1, 4)] + [along_z(k) for k in range(1, 4)]
    for other in others:
        pl.semaphore_signal(barrier, inc=1, device_id=other, device_id_type=MESH)
    outward = 2 * low_y - 1
    for s in (-1, 0, 1):
        @pl.when(exists(s, outward))
        def _(s=s):
            pl.semaphore_signal(barrier, inc=1, device_id=(slab + s, col + outward), device_id_type=MESH)

    for row in range(8):
        for comp in range(3):
            targets[row // 2 + 1, row % 2 + 1, comp * QT : (comp + 1) * QT, :] = src_ref[row, comp, 0:QT, :]
    pad_matrices(c2e_ref, m2m_ref, c2e, m2m)
    check[NS:W, :] = jnp.zeros((W - NS, 8 * W), F32)
    shifted_sources(src_ref, moved)
    acc[...] = jnp.zeros_like(acc)
    three[...] = jnp.zeros_like(three)

    more = sum(jnp.where(exists(s, outward), 1, 0) for s in (-1, 0, 1))
    pl.semaphore_wait(barrier, len(others) + more)

    def target_copy(n, s, c):
        return pltpu.make_async_remote_copy(
            src_ref=targets.at[edge(s, 4), edge(c, 2)],
            dst_ref=targets.at[border(-s, 4), border(-c, 2)],
            send_sem=t_send.at[n],
            recv_sem=t_recv.at[n],
            device_id=(slab + s, col + c),
            device_id_type=MESH,
        )

    def back_copy(n, s, c):
        return pltpu.make_async_remote_copy(
            src_ref=sums.at[border(s, 4), border(c, 2)],
            dst_ref=back.at[border(-s, 4), border(-c, 2)],
            send_sem=b_send.at[n],
            recv_sem=b_recv.at[n],
            device_id=(slab + s, col + c),
            device_id_type=MESH,
        )

    def for_sides(act):
        for n, (s, c) in enumerate(SIDES):
            @pl.when(exists(s, c))
            def _(n=n, s=s, c=c):
                act(n, s, c)

    def for_senders(act):
        for n, (s, c) in enumerate(SIDES):
            @pl.when(exists(-s, -c))
            def _(n=n, s=s, c=c):
                act(n, s, c)

    for_sides(lambda n, s, c: target_copy(n, s, c).start())

    squares_and_checks(src_ref, check, zz, yy, xx)
    part[...] = upward_two(check, c2e, m2m, grouped_up, low_y)
    theirs = pl.ds(pl.multiple_of(16 - 16 * low_y, 16), 16)
    pair_copy = pltpu.make_async_remote_copy(
        src_ref=part.at[theirs],
        dst_ref=arrived,
        send_sem=p_sem.at[0],
        recv_sem=p_sem.at[1],
        device_id=(slab, (col // 2) * 2 + 1 - low_y),
        device_id_type=MESH,
    )
    pair_copy.start()

    for_senders(lambda n, s, c: target_copy(n, s, c).wait_recv())
    pair_loop(targets, moved, acc, 0, 2, 11, 0, 6, 1)

    pair_copy.wait()
    mine = pl.ds(pl.multiple_of(16 * low_y, 16), 16)
    here = pl.ds(pl.multiple_of(8 + 16 * low_y, 8), 16)
    two[slab, col // 2, here, :] = part[mine, :] + arrived[...]

    def a_copy(k):
        block = two.at[slab, col // 2, here]
        return pltpu.make_async_remote_copy(
            src_ref=block, dst_ref=block, send_sem=a_send.at[k - 1], recv_sem=a_recv.at[k - 1],
            device_id=local_at(k), device_id_type=MESH,
        )

    def x_copy(k):
        block = two.at[:, col // 2, 8:40]
        return pltpu.make_async_remote_copy(
            src_ref=block, dst_ref=block, send_sem=x_send.at[k - 1], recv_sem=x_recv.at[k - 1],
            device_id=along_x(k), device_id_type=MESH,
        )

    def z_copy(k):
        block = two.at[:, pl.ds(zc * 4, 4), 8:40]
        return pltpu.make_async_remote_copy(
            src_ref=block, dst_ref=block, send_sem=z_send.at[k - 1], recv_sem=z_recv.at[k - 1],
            device_id=along_z(k), device_id_type=MESH,
        )

    for k in range(1, 8):
        a_copy(k).start()
    pair_loop(targets, moved, acc, 1, 10, 1, 0, 1, 5)
    for k in range(1, 8):
        a_copy(k).wait()
    for k in range(1, 4):
        x_copy(k).start()
    pair_loop(targets, moved, acc, 1, 10, 1, 5, 1, 5)

    def reduce_halo(z, y):
        sum_rows(acc, sums, z, y)

    for y in range(4):
        reduce_halo(0, y)
        reduce_halo(5, y)
    for z in range(1, 5):
        reduce_halo(z, 0)
        reduce_halo(z, 3)
    for_sides(lambda n, s, c: back_copy(n, s, c).start())
    for k in range(1, 4):
        x_copy(k).wait()
    for k in range(1, 4):
        z_copy(k).start()
    pair_loop(targets, moved, acc, 1, 10, 1, 1, 4, 1)
    for z in range(1, 5):
        for y in range(1, 3):
            sum_rows(acc, sums, z, y)
    for k in range(1, 4):
        z_copy(k).wait()

    densities_three(two, three, grouped, m2m)
    stack_sources(two, three, stacked, slab, col)
    main.wait()
    rest.wait()
    total = jnp.transpose(translate(stacked, matrix, tail))
    far2_ref[...] = total[:, 0:16]
    far3_ref[...] = 0.5 * total[:, 16:18]

    for_senders(lambda n, s, c: back_copy(n, s, c).wait_recv())
    for z in range(4):
        for y in range(2):
            value = sums[z + 1, y + 1]
            zb = {0: 0, 3: 5}.get(z)
            yb = {0: 0, 1: 3}[y]
            value = value + back[z + 1, yb]
            if zb is not None:
                value = value + back[zb, y + 1] + back[zb, yb]
            row = (z * 2 + y) * 4
            for i in range(QT):
                lines[row : row + 4, i * W : (i + 1) * W] = value[4 * i : 4 * i + 4]
    interleave(lines, near_ref)
    for_sides(lambda n, s, c: target_copy(n, s, c).wait_send())
    for_sides(lambda n, s, c: back_copy(n, s, c).wait_send())


MESH = pl.DeviceIdType.MESH
VMEM = pl.BlockSpec(memory_space=pltpu.VMEM)


def scratch(*shape, dtype=F32):
    return pltpu.VMEM(shape, dtype)


def body(offsets, charges, check_to_equiv, m2m_matrix, m2l_matrix):
    packed = jnp.concatenate([offsets, charges[:, :, None, :]], axis=2)
    sources = jnp.swapaxes(packed.reshape(8, 4, W, Q), 2, 3)
    dma = pltpu.SemaphoreType.DMA
    return pl.pallas_call(
        whole_kernel,
        name="whole",
        out_shape=(
            jax.ShapeDtypeStruct((4, 2, 4, W * QT), F32),
            jax.ShapeDtypeStruct((NS, 16), F32),
            jax.ShapeDtypeStruct((NS, 2), F32),
        ),
        in_specs=[VMEM] * 3 + [pl.BlockSpec(memory_space=pl.ANY)],
        out_specs=(VMEM, VMEM, VMEM),
        scratch_shapes=[
            scratch(6, 4, 16, W),
            scratch(6, 4, 16, W),
            scratch(6, 4, 16, 8, W),
            scratch(6, 4, 16, W),
            scratch(3, 8, 4, Q, W),
            scratch(32, QT * W),
            scratch(W, 8 * W),
            scratch(W, W),
            scratch(W, 8 * W),
            scratch(P_SIZE, Q, W),
            scratch(P_SIZE, Q, W),
            scratch(P_SIZE, Q, W),
            scratch(2, 8 * W, W, dtype=BF16),
            scratch(32, W),
            scratch(16, W),
            scratch(4, 16, 48, W),
            scratch(2, 8, 40, W),
            scratch(256, 8 * W),
            scratch(24, (K_ALL + W - 1) // W * W),
            scratch(NS, MAIN),
            scratch(NS, REST),
            dma((2,)),
            dma((8,)),
            dma((8,)),
            dma((8,)),
            dma((8,)),
            dma((2,)),
            dma((7,)),
            dma((7,)),
            dma((3,)),
            dma((3,)),
            dma((3,)),
            dma((3,)),
        ],
        compiler_params=pltpu.CompilerParams(
            vmem_limit_bytes=58 * 1024 * 1024, collective_id=0, has_side_effects=True
        ),
        cost_estimate=pl.CostEstimate(flops=400000000, bytes_accessed=16000000, transcendentals=0),
    )(sources, check_to_equiv, m2m_matrix, m2l_matrix)


def solution(mesh):
    in_specs = (P("slab", "col", None, None), P("slab", "col", None), P(), P(), P())
    out_specs = (P("slab", "col", None, None), P(None, ("slab", "col")), P(None, ("slab", "col")))
    return jax.shard_map(body, mesh=mesh, in_specs=in_specs, out_specs=out_specs, check_vma=False)
```

```python
import jax
import jax.numpy as jnp
from jax import lax
from jax.experimental import pallas as pl
from jax.experimental.pallas import tpu as pltpu
from jax.sharding import PartitionSpec as P

Q = 64
QT = 4
P_SIZE = 5
NS = 98
W = 128
SOFTEN = 0.0625
CHECK_SIDE = 1.45
F32 = jnp.float32
BF16 = jnp.bfloat16

COORD = [(float(g) / (P_SIZE - 1) - 0.5) * (2.0 * CHECK_SIDE) + 0.5 for g in range(P_SIZE)]
SURFACE = [
    (a, b, c)
    for a in range(P_SIZE)
    for b in range(P_SIZE)
    for c in range(P_SIZE)
    if min(a, b, c) == 0 or max(a, b, c) == P_SIZE - 1
]
OFFSETS = [
    (z, y, x)
    for z in range(-3, 4)
    for y in range(-3, 4)
    for x in range(-3, 4)
    if max(abs(z), abs(y), abs(x)) >= 2
]
K_ALL = len(OFFSETS) * NS
TILES = 140
CHUNK = 28 * W
LAST = K_ALL // W * W
REST = K_ALL - LAST


def split(x):
    high = x.astype(BF16)
    return high, (x - high.astype(F32)).astype(BF16)


def dot(a, b):
    return jnp.dot(a, b, preferred_element_type=F32)


def dot_t(a, b):
    return lax.dot_general(a, b, (((1,), (1,)), ((), ())), preferred_element_type=F32)


def dot3(a, b, d=dot):
    ah, al = split(a)
    bh, bl = split(b)
    return d(ah, bh) + d(ah, bl) + d(al, bh)


def squares_and_checks(src_ref, check, zz, yy, xx):
    def one_row(row, carry):
        for comp, table in ((0, zz), (1, yy), (2, xx)):
            value = src_ref[row, comp]
            for g in range(P_SIZE):
                delta = COORD[g] - value
                table[g] = delta * delta
        charge = src_ref[row, 3]
        lanes = pl.ds(pl.multiple_of(row * W, W), W)
        pair = None
        for k, (a, b, c) in enumerate(SURFACE):
            if pair != (a, b):
                pair, plane = (a, b), zz[a] + yy[b]
            term = charge * lax.rsqrt(plane + xx[c])
            check[k : k + 1, lanes] = jnp.sum(term, axis=0, keepdims=True)
        return carry

    lax.fori_loop(0, 8, one_row, 0)


def pad_matrices(c2e_ref, m2m_ref, c2e, m2m):
    c2e[...] = jnp.zeros_like(c2e)
    m2m[...] = jnp.zeros_like(m2m)
    c2e[0:NS, 0:NS] = c2e_ref[...]
    for octant in range(8):
        m2m[0:NS, octant * W : octant * W + NS] = m2m_ref[:, octant * NS : (octant + 1) * NS]


def upward_two(check, c2e, m2m, grouped, parity):
    density = dot3(c2e[...], check[...])
    high, low = split(density)
    leaf = lax.broadcasted_iota(jnp.int32, (2 * W, W), 0)
    lane = lax.broadcasted_iota(jnp.int32, (2 * W, W), 1)
    cell = (lane // 64) * W + 2 * (lane % 32) + (lane // 32) % 2
    for bx in range(2):
        pick = jnp.where(leaf == cell + 64 * bx, 1.0, 0.0).astype(BF16)
        for bz in range(2):
            for by in range(2):
                one, two = (bz * 2 + by) * W, ((bz + 2) * 2 + by) * W
                octant = 4 * bz + 2 * by + bx
                for half, part in enumerate((high, low)):
                    both = jnp.concatenate([part[:, one : one + W], part[:, two : two + W]], axis=1)
                    grouped[half, octant * W : (octant + 1) * W, :] = dot(both, pick).astype(BF16)
    mh, ml = split(m2m[...])
    level_one = dot(mh, grouped[0]) + dot(mh, grouped[1]) + dot(ml, grouped[0])
    turned = jnp.transpose(level_one)
    total = jnp.zeros((32, W), F32)
    for bz in range(2):
        for bx in range(2):
            at = pl.multiple_of((4 * bz + 2 * parity + bx) * W, W)
            block = turned[(bz * 2 + bx) * 32 : (bz * 2 + bx + 1) * 32]
            total = total + dot3(block, m2m[:, pl.ds(at, W)], dot_t)
    return total


def arrange_sources(positions, charge, moved):
    lane = lax.broadcasted_iota(jnp.int32, (Q, W), 1)

    def one(row, carry):
        z, y = row // 2, row % 2
        for comp in range(4):
            line = positions[z, comp, pl.ds(y, 1), :] if comp < 3 else charge[z, pl.ds(y, 1), :]
            turned = jnp.transpose(line.reshape(Q, W))
            value = jnp.concatenate([turned[0:Q], turned[Q : 2 * Q]], axis=1)
            half = pltpu.roll(value, 64, 1)
            left = jnp.where(lane < 64, pltpu.roll(value, 65, 1), half)
            right = jnp.where(lane < 64, half, pltpu.roll(value, 63, 1))
            if comp == 3:
                left = jnp.where(lane == 0, 0.0, left)
                right = jnp.where(lane == W - 1, 0.0, right)
            moved[0, row, comp] = left
            moved[1, row, comp] = value
            moved[2, row, comp] = right
        return carry

    lax.fori_loop(0, 8, one, 0)


def pair_rows(t_ref, moved, acc, zs, ys, sz, sy):
    tz, ty = zs + 1 - sz, ys + 1 - sy
    row = zs * 2 + ys
    centre = (sz == 0) & (sy == 0)
    sub = lax.broadcasted_iota(jnp.int32, (8, W), 0)
    rows = [jnp.broadcast_to(t_ref[tz, ty, k : k + 1, :], (8, W)) for k in range(12)]
    target_z = [rows[i] - sz.astype(F32) for i in range(QT)]
    target_y = [rows[QT + i] - sy.astype(F32) for i in range(QT)]
    sums = [jnp.zeros((8, W), F32) for _ in range(16)]
    for dx in range(3):
        target_x = [rows[2 * QT + i] - float(dx - 1) for i in range(QT)]
        for v in range(8):
            at = slice(8 * v, 8 * v + 8)
            z, y, x, q = [moved[dx, row, comp, at, :] for comp in range(4)]
            for i in range(QT):
                dz, dy, ddx = target_z[i] - z, target_y[i] - y, target_x[i] - x
                inverse = lax.rsqrt(dz * dz + dy * dy + (ddx * ddx + SOFTEN))
                weight = q * inverse
                if dx == 1 and v == 0:
                    weight = jnp.where((sub == i) & centre, 0.0, weight)
                cubed = weight * (inverse * inverse)
                sums[4 * i] += weight
                sums[4 * i + 1] += cubed * dz
                sums[4 * i + 2] += cubed * dy
                sums[4 * i + 3] += cubed * ddx
    for k in range(16):
        acc[tz, ty, k] += sums[k]


def pair_loop(t_ref, moved, acc, z_first, z_count, z_step, y_first, y_count, y_step=1):
    def one(p, carry):
        iz, iy = z_first + z_step * (p // y_count), y_first + y_step * (p % y_count)
        pair_rows(t_ref, moved, acc, iz // 3, iy // 3, 1 - iz % 3, 1 - iy % 3)
        return carry

    lax.fori_loop(0, z_count * y_count, one, 0, unroll=2)


def sum_rows(acc, sums, z, y):
    sums[z, y] = jnp.sum(acc[z, y], axis=1)


def densities_three(two, three, grouped, m2m):
    def gather(n, carry):
        z, y = n // 8, n % 8
        for bz in range(2):
            for by in range(2):
                for bx in range(2):
                    octant = 4 * bz + 2 * by + bx
                    grouped[pl.ds(pl.multiple_of(n * 16, 16), 16), octant * W : (octant + 1) * W] = two[
                        2 * z + bz, 2 * y + by, pl.ds(8 + bx, 16, stride=2), :
                    ]
        return carry

    lax.fori_loop(0, 16, gather, 0)
    level_three = dot3(grouped[...], m2m[...], dot_t)
    for n in range(16):
        three[n // 8, n % 8, 8:24, :] = level_three[n * 16 : (n + 1) * 16]


def stack_sources(two, three, stacked, slab, col):
    z2, y2, x2 = slab, col // 2, 16 * (col % 2)
    z3, y3, x3 = slab // 2, 4 * (slab % 2) + col // 8, 2 * (col % 8)
    sub = lax.broadcasted_iota(jnp.int32, (24, W), 0)
    lane = lax.broadcasted_iota(jnp.int32, (24, W), 1)

    def use(cell, shift, size):
        at = cell + shift
        near = jnp.abs(at // 2 - cell // 2) <= 1
        return (at >= 0) & (at < size) & near, jnp.clip(at, 0, size - 1)

    for gz in range(-3, 4):
        chosen = [o for o, shift in enumerate(OFFSETS) if shift[0] == gz]

        @pl.when((slab + gz >= 0) & (slab + gz < 4))
        def _(chosen=chosen):
            pending = None
            for o in chosen:
                _, oy, ox = OFFSETS[o]
                oz = OFFSETS[o][0]
                uz2, sz2 = use(z2, oz, 4)
                uy2, sy2 = use(y2, oy, 16)
                uz3, sz3 = use(z3, oz, 2)
                uy3, sy3 = use(y3, oy, 8)
                keep2 = jnp.where(uz2 & uy2, 1.0, 0.0).astype(F32)
                keep3 = jnp.where(uz3 & uy3, 1.0, 0.0).astype(F32)
                value = jnp.concatenate(
                    [
                        two[sz2, sy2, pl.ds(8 + x2 + ox, 16), :] * keep2,
                        three[sz3, sy3, pl.ds(8 + x3 + ox, 8), :] * keep3,
                    ],
                    axis=0,
                )
                if ox == 3:
                    value = jnp.where(sub % 2 == 0, value, 0.0)
                if ox == -3:
                    value = jnp.where(sub % 2 == 1, value, 0.0)
                tile, start = divmod(o * NS, W)
                at = slice(tile * W, (tile + 1) * W)
                if start:
                    value = pltpu.roll(value, start, 1)
                    if pending is None:
                        pending = stacked[:, at]
                    filled = jnp.where(lane < start, pending, value)
                else:
                    filled = value
                if start + NS >= W:
                    stacked[:, at] = filled
                    pending = value if start + NS > W else None
                else:
                    pending = filled
            if pending is not None:
                tile, end = divmod((chosen[-1] + 1) * NS, W)
                stacked[:, tile * W : (tile + 1) * W] = jnp.where(lane < end, pending, 0.0)


def far_terms(matrix, sources):
    mh, ml = split(matrix)
    sh, sl = split(sources)
    return dot_t(mh, jnp.concatenate([sh, sl], axis=0)) + dot_t(ml, jnp.concatenate([sh, jnp.zeros_like(sl)], axis=0))


def translate(stacked, matrix, tail, first):
    def one(n, total):
        here = pl.ds(pl.multiple_of(n * CHUNK, W), CHUNK)
        there = pl.ds(pl.multiple_of(first + n * CHUNK, W), CHUNK)
        return total + far_terms(matrix[:, here], stacked[:, there])

    total = far_terms(tail[...], stacked[:, LAST:K_ALL])
    total = lax.fori_loop(0, TILES * W // CHUNK, one, total)
    return total[:, 0:24] + total[:, 24:48]


def finish_kernel(lines, far, out_ref, far2_ref, far3_ref):
    far2_ref[...] = far[0:16]
    far3_ref[...] = 0.5 * far[16:18]
    source = lax.broadcasted_iota(jnp.int32, (QT * W, QT * W), 0)
    place = lax.broadcasted_iota(jnp.int32, (QT * W, QT * W), 1)
    move = jnp.where(place == QT * (2 * (source % 64) + source // 64 % 2) + source // W, 1.0, 0.0).astype(BF16)
    value = lines[...]
    high, low = split(value)
    lowest = (value - high.astype(F32) - low.astype(F32)).astype(BF16)
    result = dot(high, move) + dot(low, move) + dot(lowest, move)
    for row in range(8):
        out_ref[row // 2, row % 2] = result[4 * row : 4 * row + 4]


SIDES = [(s, c) for s in (-1, 0, 1) for c in (-1, 0, 1) if (s, c) != (0, 0)]


def border(step, size):
    return {-1: slice(0, 1), 0: slice(1, size + 1), 1: slice(size + 1, size + 2)}[step]


def edge(step, size):
    return {-1: slice(1, 2), 0: slice(1, size + 1), 1: slice(size, size + 1)}[step]


def whole_kernel(
    positions_ref, charges_ref, c2e_ref, m2m_ref, m2l_ref, lines, far,
    positions, charge, c2e_in, m2m_in, targets, back, acc, sums, moved, m2m, c2e, check, zz, yy, xx, grouped_up,
    part, arrived, two, three, grouped, stacked, matrix, tail,
    load_sem, t_send, t_recv, b_send, b_recv, p_sem, a_send, a_recv, x_send, x_recv, z_send, z_recv,
):
    slab, col = lax.axis_index("slab"), lax.axis_index("col")
    zc, xc, low_y = col // 8, (col // 2) % 4, col % 2
    place = slab * 2 + low_y

    def local_at(k):
        to = lax.rem(place + k, 8)
        return to // 2, (col // 2) * 2 + lax.rem(to, 2)

    def along_x(k):
        return slab, zc * 8 + lax.rem(xc + k, 4) * 2 + low_y

    def along_z(k):
        return slab, lax.rem(zc + k, 4) * 8 + xc * 2 + low_y

    def exists(s, c):
        return (slab + s >= 0) & (slab + s < 4) & (col + c >= 0) & (col + c < 32)

    first = pl.multiple_of(W * (35 * (3 - slab) - jnp.where(slab == 0, 4, 0)), W)
    loads = [
        pltpu.make_async_copy(positions_ref, positions, load_sem.at[0]),
        pltpu.make_async_copy(charges_ref, charge, load_sem.at[1]),
        pltpu.make_async_copy(c2e_ref, c2e_in, load_sem.at[2]),
        pltpu.make_async_copy(m2m_ref, m2m_in, load_sem.at[3]),
        pltpu.make_async_copy(m2l_ref.at[:, pl.ds(first, TILES * W)], matrix, load_sem.at[4]),
        pltpu.make_async_copy(m2l_ref.at[:, pl.ds(LAST, REST)], tail, load_sem.at[5]),
    ]
    for load in loads:
        load.start()

    targets[...] = jnp.zeros_like(targets)
    back[...] = jnp.zeros_like(back)
    two[:, :, 0:8, :] = jnp.zeros((4, 16, 8, W), F32)
    two[:, :, 40:48, :] = jnp.zeros((4, 16, 8, W), F32)

    barrier = pltpu.get_barrier_semaphore()
    others = [local_at(k) for k in range(1, 8)]
    others += [along_x(k) for k in range(1, 4)] + [along_z(k) for k in range(1, 4)]
    for other in others:
        pl.semaphore_signal(barrier, inc=1, device_id=other, device_id_type=MESH)
    outward = 2 * low_y - 1
    for s in (-1, 0, 1):
        @pl.when(exists(s, outward))
        def _(s=s):
            pl.semaphore_signal(barrier, inc=1, device_id=(slab + s, col + outward), device_id_type=MESH)

    three[...] = jnp.zeros_like(three)
    acc[...] = jnp.zeros_like(acc)
    stacked[...] = jnp.zeros_like(stacked)
    check[NS:W, :] = jnp.zeros((W - NS, 8 * W), F32)
    loads[0].wait()
    loads[1].wait()
    arrange_sources(positions, charge, moved)
    for row in range(8):
        for comp in range(3):
            targets[row // 2 + 1, row % 2 + 1, comp * QT : (comp + 1) * QT, :] = moved[1, row, comp, 0:QT, :]
    loads[2].wait()
    loads[3].wait()
    pad_matrices(c2e_in, m2m_in, c2e, m2m)

    more = sum(jnp.where(exists(s, outward), 1, 0) for s in (-1, 0, 1))
    pl.semaphore_wait(barrier, len(others) + more)

    def target_copy(n, s, c):
        return pltpu.make_async_remote_copy(
            src_ref=targets.at[edge(s, 4), edge(c, 2)],
            dst_ref=targets.at[border(-s, 4), border(-c, 2)],
            send_sem=t_send.at[n],
            recv_sem=t_recv.at[n],
            device_id=(slab + s, col + c),
            device_id_type=MESH,
        )

    def back_copy(n, s, c):
        return pltpu.make_async_remote_copy(
            src_ref=sums.at[border(s, 4), border(c, 2)],
            dst_ref=back.at[border(-s, 4), border(-c, 2)],
            send_sem=b_send.at[n],
            recv_sem=b_recv.at[n],
            device_id=(slab + s, col + c),
            device_id_type=MESH,
        )

    def for_sides(act):
        for n, (s, c) in enumerate(SIDES):
            @pl.when(exists(s, c))
            def _(n=n, s=s, c=c):
                act(n, s, c)

    def for_senders(act):
        for n, (s, c) in enumerate(SIDES):
            @pl.when(exists(-s, -c))
            def _(n=n, s=s, c=c):
                act(n, s, c)

    for_sides(lambda n, s, c: target_copy(n, s, c).start())

    squares_and_checks(moved.at[1], check, zz, yy, xx)
    part[...] = upward_two(check, c2e, m2m, grouped_up, low_y)
    theirs = pl.ds(pl.multiple_of(16 - 16 * low_y, 16), 16)
    pair_copy = pltpu.make_async_remote_copy(
        src_ref=part.at[theirs],
        dst_ref=arrived,
        send_sem=p_sem.at[0],
        recv_sem=p_sem.at[1],
        device_id=(slab, (col // 2) * 2 + 1 - low_y),
        device_id_type=MESH,
    )
    pair_copy.start()

    for_senders(lambda n, s, c: target_copy(n, s, c).wait_recv())
    pair_loop(targets, moved, acc, 0, 1, 1, 0, 6)

    pair_copy.wait()
    mine = pl.ds(pl.multiple_of(16 * low_y, 16), 16)
    here = pl.ds(pl.multiple_of(8 + 16 * low_y, 8), 16)
    two[slab, col // 2, here, :] = part[mine, :] + arrived[...]

    def a_copy(k):
        block = two.at[slab, col // 2, here]
        return pltpu.make_async_remote_copy(
            src_ref=block, dst_ref=block, send_sem=a_send.at[k - 1], recv_sem=a_recv.at[k - 1],
            device_id=local_at(k), device_id_type=MESH,
        )

    def x_copy(k):
        block = two.at[:, col // 2, 8:40]
        return pltpu.make_async_remote_copy(
            src_ref=block, dst_ref=block, send_sem=x_send.at[k - 1], recv_sem=x_recv.at[k - 1],
            device_id=along_x(k), device_id_type=MESH,
        )

    def z_copy(k):
        block = two.at[:, pl.ds(zc * 4, 4), 8:40]
        return pltpu.make_async_remote_copy(
            src_ref=block, dst_ref=block, send_sem=z_send.at[k - 1], recv_sem=z_recv.at[k - 1],
            device_id=along_z(k), device_id_type=MESH,
        )

    for k in range(1, 8):
        a_copy(k).start()
    pair_loop(targets, moved, acc, 11, 1, 1, 0, 6)
    for k in range(1, 8):
        a_copy(k).wait()
    for k in range(1, 4):
        x_copy(k).start()
    pair_loop(targets, moved, acc, 1, 10, 1, 0, 1)
    for k in range(1, 4):
        x_copy(k).wait()
    for k in range(1, 4):
        z_copy(k).start()
    pair_loop(targets, moved, acc, 1, 10, 1, 5, 1)

    def reduce_halo(z, y):
        sum_rows(acc, sums, z, y)

    for y in range(4):
        reduce_halo(0, y)
        reduce_halo(5, y)
    for z in range(1, 5):
        reduce_halo(z, 0)
        reduce_halo(z, 3)
    for_sides(lambda n, s, c: back_copy(n, s, c).start())
    pair_loop(targets, moved, acc, 1, 10, 1, 1, 4)
    for z in range(1, 5):
        for y in range(1, 3):
            sum_rows(acc, sums, z, y)
    for k in range(1, 4):
        z_copy(k).wait()

    densities_three(two, three, grouped, m2m)
    stack_sources(two, three, stacked, slab, col)
    loads[4].wait()
    loads[5].wait()
    far[...] = jnp.transpose(translate(stacked, matrix, tail, first))

    for_senders(lambda n, s, c: back_copy(n, s, c).wait_recv())
    for z in range(4):
        for y in range(2):
            value = sums[z + 1, y + 1]
            zb = {0: 0, 3: 5}.get(z)
            yb = {0: 0, 1: 3}[y]
            value = value + back[z + 1, yb]
            if zb is not None:
                value = value + back[zb, y + 1] + back[zb, yb]
            row = (z * 2 + y) * 4
            for i in range(QT):
                lines[row : row + 4, i * W : (i + 1) * W] = value[4 * i : 4 * i + 4]
    for_sides(lambda n, s, c: target_copy(n, s, c).wait_send())
    for_sides(lambda n, s, c: back_copy(n, s, c).wait_send())


MESH = pl.DeviceIdType.MESH
VMEM = pl.BlockSpec(memory_space=pltpu.VMEM)


def scratch(*shape, dtype=F32):
    return pltpu.VMEM(shape, dtype)


def body(offsets, charges, check_to_equiv, m2m_matrix, m2l_matrix):
    dma = pltpu.SemaphoreType.DMA
    lines, far = pl.pallas_call(
        whole_kernel,
        name="whole",
        out_shape=(
            jax.ShapeDtypeStruct((32, W * QT), F32),
            jax.ShapeDtypeStruct((24, NS), F32),
        ),
        in_specs=[pl.BlockSpec(memory_space=pl.ANY)] * 5,
        out_specs=(VMEM, VMEM),
        scratch_shapes=[
            scratch(4, 3, 2, W * Q),
            scratch(4, 2, W * Q),
            scratch(NS, NS),
            scratch(NS, 8 * NS),
            scratch(6, 4, 16, W),
            scratch(6, 4, 16, W),
            scratch(6, 4, 16, 8, W),
            scratch(6, 4, 16, W),
            scratch(3, 8, 4, Q, W),
            scratch(W, 8 * W),
            scratch(W, W),
            scratch(W, 8 * W),
            scratch(P_SIZE, Q, W),
            scratch(P_SIZE, Q, W),
            scratch(P_SIZE, Q, W),
            scratch(2, 8 * W, W, dtype=BF16),
            scratch(32, W),
            scratch(16, W),
            scratch(4, 16, 48, W),
            scratch(2, 8, 40, W),
            scratch(256, 8 * W),
            scratch(24, (K_ALL + W - 1) // W * W),
            scratch(NS, TILES * W),
            scratch(NS, REST),
            dma((6,)),
            dma((8,)),
            dma((8,)),
            dma((8,)),
            dma((8,)),
            dma((2,)),
            dma((7,)),
            dma((7,)),
            dma((3,)),
            dma((3,)),
            dma((3,)),
            dma((3,)),
        ],
        compiler_params=pltpu.CompilerParams(
            vmem_limit_bytes=58 * 1024 * 1024, collective_id=0, has_side_effects=True
        ),
        cost_estimate=pl.CostEstimate(flops=400000000, bytes_accessed=16000000, transcendentals=0),
    )(jnp.swapaxes(offsets, 1, 2), charges, check_to_equiv, m2m_matrix, m2l_matrix)
    near_field, far2, far3 = pl.pallas_call(
        finish_kernel,
        name="finish",
        out_shape=(
            jax.ShapeDtypeStruct((4, 2, 4, W * QT), F32),
            jax.ShapeDtypeStruct((16, NS), F32),
            jax.ShapeDtypeStruct((2, NS), F32),
        ),
        in_specs=[VMEM, VMEM],
        out_specs=(VMEM, VMEM, VMEM),
    )(lines, far)
    return near_field, jnp.transpose(far2), jnp.transpose(far3)


def solution(mesh):
    in_specs = (P("slab", "col", None, None), P("slab", "col", None), P(), P(), P())
    out_specs = (P("slab", "col", None, None), P(None, ("slab", "col")), P(None, ("slab", "col")))
    return jax.shard_map(body, mesh=mesh, in_specs=in_specs, out_specs=out_specs, check_vma=False)
```

```python
import jax
import jax.numpy as jnp
from jax import lax
from jax.experimental import pallas as pl
from jax.experimental.pallas import tpu as pltpu
from jax.sharding import PartitionSpec as P

Q = 64
QT = 4
P_SIZE = 5
NS = 98
W = 128
SOFTEN = 0.0625
CHECK_SIDE = 1.45
F32 = jnp.float32
BF16 = jnp.bfloat16

COORD = [(float(g) / (P_SIZE - 1) - 0.5) * (2.0 * CHECK_SIDE) + 0.5 for g in range(P_SIZE)]
SURFACE = [
    (a, b, c)
    for a in range(P_SIZE)
    for b in range(P_SIZE)
    for c in range(P_SIZE)
    if min(a, b, c) == 0 or max(a, b, c) == P_SIZE - 1
]
OFFSETS = [
    (z, y, x)
    for z in range(-3, 4)
    for y in range(-3, 4)
    for x in range(-3, 4)
    if max(abs(z), abs(y), abs(x)) >= 2
]
K_ALL = len(OFFSETS) * NS
TILES = 140
CHUNK = 28 * W
LAST = K_ALL // W * W
REST = K_ALL - LAST


def split(x):
    high = x.astype(BF16)
    return high, (x - high.astype(F32)).astype(BF16)


def dot(a, b):
    return jnp.dot(a, b, preferred_element_type=F32)


def dot_t(a, b):
    return lax.dot_general(a, b, (((1,), (1,)), ((), ())), preferred_element_type=F32)


def dot3(a, b, d=dot):
    ah, al = split(a)
    bh, bl = split(b)
    return d(ah, bh) + d(ah, bl) + d(al, bh)


def squares_and_checks(src_ref, check, zz, yy, xx):
    def one_row(row, carry):
        for comp, table in ((0, zz), (1, yy), (2, xx)):
            value = src_ref[row, comp]
            for g in range(P_SIZE):
                delta = COORD[g] - value
                table[g] = delta * delta
        charge = src_ref[row, 3]
        lanes = pl.ds(pl.multiple_of(row * W, W), W)
        pair = None
        for k, (a, b, c) in enumerate(SURFACE):
            if pair != (a, b):
                pair, plane = (a, b), zz[a] + yy[b]
            term = charge * lax.rsqrt(plane + xx[c])
            check[k : k + 1, lanes] = jnp.sum(term, axis=0, keepdims=True)
        return carry

    lax.fori_loop(0, 8, one_row, 0)


def pad_matrices(c2e_ref, m2m_ref, c2e, m2m):
    c2e[...] = jnp.zeros_like(c2e)
    m2m[...] = jnp.zeros_like(m2m)
    c2e[0:NS, 0:NS] = c2e_ref[...]
    for octant in range(8):
        m2m[0:NS, octant * W : octant * W + NS] = m2m_ref[:, octant * NS : (octant + 1) * NS]


def upward_two(check, c2e, m2m, grouped, parity):
    density = dot3(c2e[...], check[...])
    high, low = split(density)
    leaf = lax.broadcasted_iota(jnp.int32, (2 * W, W), 0)
    lane = lax.broadcasted_iota(jnp.int32, (2 * W, W), 1)
    cell = (lane // 64) * W + 2 * (lane % 32) + (lane // 32) % 2
    for bx in range(2):
        pick = jnp.where(leaf == cell + 64 * bx, 1.0, 0.0).astype(BF16)
        for bz in range(2):
            for by in range(2):
                one, two = (bz * 2 + by) * W, ((bz + 2) * 2 + by) * W
                octant = 4 * bz + 2 * by + bx
                for half, part in enumerate((high, low)):
                    both = jnp.concatenate([part[:, one : one + W], part[:, two : two + W]], axis=1)
                    grouped[half, octant * W : (octant + 1) * W, :] = dot(both, pick).astype(BF16)
    mh, ml = split(m2m[...])
    level_one = dot(mh, grouped[0]) + dot(mh, grouped[1]) + dot(ml, grouped[0])
    turned = jnp.transpose(level_one)
    total = jnp.zeros((32, W), F32)
    for bz in range(2):
        for bx in range(2):
            at = pl.multiple_of((4 * bz + 2 * parity + bx) * W, W)
            block = turned[(bz * 2 + bx) * 32 : (bz * 2 + bx + 1) * 32]
            total = total + dot3(block, m2m[:, pl.ds(at, W)], dot_t)
    return total


def arrange_sources(positions, charge, moved):
    lane = lax.broadcasted_iota(jnp.int32, (Q, W), 1)

    def one(row, carry):
        z, y = row // 2, row % 2
        for comp in range(4):
            line = positions[z, comp, pl.ds(y, 1), :] if comp < 3 else charge[z, pl.ds(y, 1), :]
            turned = jnp.transpose(line.reshape(Q, W))
            value = jnp.concatenate([turned[0:Q], turned[Q : 2 * Q]], axis=1)
            half = pltpu.roll(value, 64, 1)
            left = jnp.where(lane < 64, pltpu.roll(value, 65, 1), half)
            right = jnp.where(lane < 64, half, pltpu.roll(value, 63, 1))
            if comp == 3:
                left = jnp.where(lane == 0, 0.0, left)
                right = jnp.where(lane == W - 1, 0.0, right)
            moved[0, row, comp] = left
            moved[1, row, comp] = value
            moved[2, row, comp] = right
        return carry

    lax.fori_loop(0, 8, one, 0)


def pair_rows(t_ref, moved, acc, zs, ys, sz, sy):
    tz, ty = zs + 1 - sz, ys + 1 - sy
    row = zs * 2 + ys
    centre = (sz == 0) & (sy == 0)
    sub = lax.broadcasted_iota(jnp.int32, (8, W), 0)
    rows = [jnp.broadcast_to(t_ref[tz, ty, k : k + 1, :], (8, W)) for k in range(12)]
    target_z = [rows[i] - sz.astype(F32) for i in range(QT)]
    target_y = [rows[QT + i] - sy.astype(F32) for i in range(QT)]
    sums = [jnp.zeros((8, W), F32) for _ in range(16)]
    for dx in range(3):
        target_x = [rows[2 * QT + i] - float(dx - 1) for i in range(QT)]
        for v in range(8):
            at = slice(8 * v, 8 * v + 8)
            z, y, x, q = [moved[dx, row, comp, at, :] for comp in range(4)]
            for i in range(QT):
                dz, dy, ddx = target_z[i] - z, target_y[i] - y, target_x[i] - x
                inverse = lax.rsqrt(dz * dz + dy * dy + (ddx * ddx + SOFTEN))
                weight = q * inverse
                if dx == 1 and v == 0:
                    weight = jnp.where((sub == i) & centre, 0.0, weight)
                cubed = weight * (inverse * inverse)
                sums[4 * i] += weight
                sums[4 * i + 1] += cubed * dz
                sums[4 * i + 2] += cubed * dy
                sums[4 * i + 3] += cubed * ddx
    for k in range(16):
        acc[tz, ty, k] += sums[k]


def pair_loop(t_ref, moved, acc, z_first, z_count, z_step, y_first, y_count, y_step=1):
    def one(p, carry):
        iz, iy = z_first + z_step * (p // y_count), y_first + y_step * (p % y_count)
        pair_rows(t_ref, moved, acc, iz // 3, iy // 3, 1 - iz % 3, 1 - iy % 3)
        return carry

    lax.fori_loop(0, z_count * y_count, one, 0, unroll=2)


def sum_rows(acc, sums, z, y):
    sums[z, y] = jnp.sum(acc[z, y], axis=1)


def densities_three(two, three, grouped, m2m, zc):
    for n in range(4):
        z, y = n // 2, 2 * zc + n % 2
        for octant in range(8):
            bz, by, bx = octant // 4, octant // 2 % 2, octant % 2
            grouped[n * 16 : (n + 1) * 16, octant * W : (octant + 1) * W] = two[
                2 * z + bz, 2 * y + by, pl.ds(8 + bx, 16, stride=2), :
            ]
    level_three = dot3(grouped[...], m2m[...], dot_t)
    for n in range(4):
        three[n // 2, 2 * zc + n % 2, 8:24, :] = level_three[n * 16 : (n + 1) * 16]


def stack_sources(two, three, stacked, slab, col):
    z2, y2, x2 = slab, col // 2, 16 * (col % 2)
    z3, y3, x3 = slab // 2, 4 * (slab % 2) + col // 8, 2 * (col % 8)
    sub = lax.broadcasted_iota(jnp.int32, (24, W), 0)
    lane = lax.broadcasted_iota(jnp.int32, (24, W), 1)

    def use(cell, shift, size):
        at = cell + shift
        near = jnp.abs(at // 2 - cell // 2) <= 1
        return (at >= 0) & (at < size) & near, jnp.clip(at, 0, size - 1)

    for gz in range(-3, 4):
        chosen = [o for o, shift in enumerate(OFFSETS) if shift[0] == gz]

        @pl.when((slab + gz >= 0) & (slab + gz < 4))
        def _(chosen=chosen):
            pending = None
            for o in chosen:
                _, oy, ox = OFFSETS[o]
                oz = OFFSETS[o][0]
                uz2, sz2 = use(z2, oz, 4)
                uy2, sy2 = use(y2, oy, 16)
                uz3, sz3 = use(z3, oz, 2)
                uy3, sy3 = use(y3, oy, 8)
                keep2 = jnp.where(uz2 & uy2, 1.0, 0.0).astype(F32)
                keep3 = jnp.where(uz3 & uy3, 1.0, 0.0).astype(F32)
                value = jnp.concatenate(
                    [
                        two[sz2, sy2, pl.ds(8 + x2 + ox, 16), :] * keep2,
                        three[sz3, sy3, pl.ds(8 + x3 + ox, 8), :] * keep3,
                    ],
                    axis=0,
                )
                if ox == 3:
                    value = jnp.where(sub % 2 == 0, value, 0.0)
                if ox == -3:
                    value = jnp.where(sub % 2 == 1, value, 0.0)
                tile, start = divmod(o * NS, W)
                at = slice(tile * W, (tile + 1) * W)
                if start:
                    value = pltpu.roll(value, start, 1)
                    if pending is None:
                        pending = stacked[:, at]
                    filled = jnp.where(lane < start, pending, value)
                else:
                    filled = value
                if start + NS >= W:
                    stacked[:, at] = filled
                    pending = value if start + NS > W else None
                else:
                    pending = filled
            if pending is not None:
                tile, end = divmod((chosen[-1] + 1) * NS, W)
                stacked[:, tile * W : (tile + 1) * W] = jnp.where(lane < end, pending, 0.0)


def far_terms(matrix, sources):
    mh, ml = split(matrix)
    sh, sl = split(sources)
    return dot_t(mh, jnp.concatenate([sh, sl], axis=0)) + dot_t(ml, jnp.concatenate([sh, jnp.zeros_like(sl)], axis=0))


def translate(stacked, matrix, tail, first):
    def one(n, total):
        here = pl.ds(pl.multiple_of(n * CHUNK, W), CHUNK)
        there = pl.ds(pl.multiple_of(first + n * CHUNK, W), CHUNK)
        return total + far_terms(matrix[:, here], stacked[:, there])

    total = far_terms(tail[...], stacked[:, LAST:K_ALL])
    total = lax.fori_loop(0, TILES * W // CHUNK, one, total)
    return total[:, 0:24] + total[:, 24:48]


def finish_kernel(lines, far, out_ref, far2_ref, far3_ref):
    far2_ref[...] = far[0:16]
    far3_ref[...] = 0.5 * far[16:18]
    source = lax.broadcasted_iota(jnp.int32, (QT * W, QT * W), 0)
    place = lax.broadcasted_iota(jnp.int32, (QT * W, QT * W), 1)
    move = jnp.where(place == QT * (2 * (source % 64) + source // 64 % 2) + source // W, 1.0, 0.0).astype(BF16)
    value = lines[...]
    high, low = split(value)
    lowest = (value - high.astype(F32) - low.astype(F32)).astype(BF16)
    result = dot(high, move) + dot(low, move) + dot(lowest, move)
    for row in range(8):
        out_ref[row // 2, row % 2] = result[4 * row : 4 * row + 4]


SIDES = [(s, c) for s in (-1, 0, 1) for c in (-1, 0, 1) if (s, c) != (0, 0)]


def border(step, size):
    return {-1: slice(0, 1), 0: slice(1, size + 1), 1: slice(size + 1, size + 2)}[step]


def edge(step, size):
    return {-1: slice(1, 2), 0: slice(1, size + 1), 1: slice(size, size + 1)}[step]


def whole_kernel(
    positions_ref, charges_ref, c2e_ref, m2m_ref, m2l_ref, lines, far,
    positions, charge, c2e_in, m2m_in, targets, back, acc, sums, moved, m2m, c2e, check, zz, yy, xx, grouped_up,
    part, arrived, two, three, grouped, stacked, matrix, tail,
    load_sem, t_send, t_recv, b_send, b_recv, p_sem, a_send, a_recv, x_send, x_recv, z_send, z_recv,
    up_send, up_recv, down_send, down_recv,
):
    slab, col = lax.axis_index("slab"), lax.axis_index("col")
    zc, xc, low_y = col // 8, (col // 2) % 4, col % 2
    place = slab * 2 + low_y

    def local_at(k):
        to = lax.rem(place + k, 8)
        return to // 2, (col // 2) * 2 + lax.rem(to, 2)

    def along_x(k):
        return slab, zc * 8 + lax.rem(xc + k, 4) * 2 + low_y

    def along_z(k):
        return slab, lax.rem(zc + k, 4) * 8 + xc * 2 + low_y

    def exists(s, c):
        return (slab + s >= 0) & (slab + s < 4) & (col + c >= 0) & (col + c < 32)

    first = pl.multiple_of(W * (35 * (3 - slab) - jnp.where(slab == 0, 4, 0)), W)
    loads = [
        pltpu.make_async_copy(positions_ref, positions, load_sem.at[0]),
        pltpu.make_async_copy(charges_ref, charge, load_sem.at[1]),
        pltpu.make_async_copy(c2e_ref, c2e_in, load_sem.at[2]),
        pltpu.make_async_copy(m2m_ref, m2m_in, load_sem.at[3]),
        pltpu.make_async_copy(m2l_ref.at[:, pl.ds(first, TILES * W)], matrix, load_sem.at[4]),
        pltpu.make_async_copy(m2l_ref.at[:, pl.ds(LAST, REST)], tail, load_sem.at[5]),
    ]
    for load in loads:
        load.start()

    targets[...] = jnp.zeros_like(targets)
    back[...] = jnp.zeros_like(back)
    three[...] = jnp.zeros_like(three)
    two[:, :, 0:8, :] = jnp.zeros((4, 16, 8, W), F32)
    two[:, :, 40:48, :] = jnp.zeros((4, 16, 8, W), F32)

    barrier = pltpu.get_barrier_semaphore()
    others = [local_at(k) for k in range(1, 8)]
    others += [along_x(k) for k in range(1, 4)] + [along_z(k) for k in range(1, 4)]
    for other in others:
        pl.semaphore_signal(barrier, inc=1, device_id=other, device_id_type=MESH)
    outward = 2 * low_y - 1
    for s in (-1, 0, 1):
        @pl.when(exists(s, outward))
        def _(s=s):
            pl.semaphore_signal(barrier, inc=1, device_id=(slab + s, col + outward), device_id_type=MESH)

    acc[...] = jnp.zeros_like(acc)
    stacked[...] = jnp.zeros_like(stacked)
    check[NS:W, :] = jnp.zeros((W - NS, 8 * W), F32)
    loads[0].wait()
    loads[1].wait()
    arrange_sources(positions, charge, moved)
    for row in range(8):
        for comp in range(3):
            targets[row // 2 + 1, row % 2 + 1, comp * QT : (comp + 1) * QT, :] = moved[1, row, comp, 0:QT, :]
    loads[2].wait()
    loads[3].wait()
    pad_matrices(c2e_in, m2m_in, c2e, m2m)

    more = sum(jnp.where(exists(s, outward), 1, 0) for s in (-1, 0, 1))
    pl.semaphore_wait(barrier, len(others) + more)

    def target_copy(n, s, c):
        return pltpu.make_async_remote_copy(
            src_ref=targets.at[edge(s, 4), edge(c, 2)],
            dst_ref=targets.at[border(-s, 4), border(-c, 2)],
            send_sem=t_send.at[n],
            recv_sem=t_recv.at[n],
            device_id=(slab + s, col + c),
            device_id_type=MESH,
        )

    def back_copy(n, s, c):
        return pltpu.make_async_remote_copy(
            src_ref=sums.at[border(s, 4), border(c, 2)],
            dst_ref=back.at[border(-s, 4), border(-c, 2)],
            send_sem=b_send.at[n],
            recv_sem=b_recv.at[n],
            device_id=(slab + s, col + c),
            device_id_type=MESH,
        )

    def for_sides(act):
        for n, (s, c) in enumerate(SIDES):
            @pl.when(exists(s, c))
            def _(n=n, s=s, c=c):
                act(n, s, c)

    def for_senders(act):
        for n, (s, c) in enumerate(SIDES):
            @pl.when(exists(-s, -c))
            def _(n=n, s=s, c=c):
                act(n, s, c)

    for_sides(lambda n, s, c: target_copy(n, s, c).start())

    squares_and_checks(moved.at[1], check, zz, yy, xx)
    part[...] = upward_two(check, c2e, m2m, grouped_up, low_y)
    theirs = pl.ds(pl.multiple_of(16 - 16 * low_y, 16), 16)
    pair_copy = pltpu.make_async_remote_copy(
        src_ref=part.at[theirs],
        dst_ref=arrived,
        send_sem=p_sem.at[0],
        recv_sem=p_sem.at[1],
        device_id=(slab, (col // 2) * 2 + 1 - low_y),
        device_id_type=MESH,
    )
    pair_copy.start()

    for_senders(lambda n, s, c: target_copy(n, s, c).wait_recv())
    pair_loop(targets, moved, acc, 0, 1, 1, 0, 6)

    pair_copy.wait()
    mine = pl.ds(pl.multiple_of(16 * low_y, 16), 16)
    here = pl.ds(pl.multiple_of(8 + 16 * low_y, 8), 16)
    two[slab, col // 2, here, :] = part[mine, :] + arrived[...]

    def a_copy(k):
        block = two.at[slab, col // 2, here]
        return pltpu.make_async_remote_copy(
            src_ref=block, dst_ref=block, send_sem=a_send.at[k - 1], recv_sem=a_recv.at[k - 1],
            device_id=local_at(k), device_id_type=MESH,
        )

    def x_copy(k):
        block = two.at[:, col // 2, 8:40]
        return pltpu.make_async_remote_copy(
            src_ref=block, dst_ref=block, send_sem=x_send.at[k - 1], recv_sem=x_recv.at[k - 1],
            device_id=along_x(k), device_id_type=MESH,
        )

    def z_copy(k):
        block = three.at[:, pl.ds(2 * zc, 2), 8:24]
        return pltpu.make_async_remote_copy(
            src_ref=block, dst_ref=block, send_sem=z_send.at[k - 1], recv_sem=z_recv.at[k - 1],
            device_id=along_z(k), device_id_type=MESH,
        )

    def row_copy(r, step):
        send, recv = (up_send, up_recv) if step == 1 else (down_send, down_recv)
        block = two.at[:, zc * 4 + r, 8:40]
        return pltpu.make_async_remote_copy(
            src_ref=block, dst_ref=block, send_sem=send.at[r], recv_sem=recv.at[r],
            device_id=(slab, col + 8 * step), device_id_type=MESH,
        )

    def for_rows(act, sender):
        for r in range(4):
            if r > 0:
                @pl.when((r > xc) & ((zc < 3) if sender else (zc > 0)))
                def _(r=r):
                    act(row_copy(r, 1))
            if r < 3:
                @pl.when((r < xc) & ((zc > 0) if sender else (zc < 3)))
                def _(r=r):
                    act(row_copy(r, -1))

    for k in range(1, 8):
        a_copy(k).start()
    pair_loop(targets, moved, acc, 11, 1, 1, 0, 6)
    pair_loop(targets, moved, acc, 1, 10, 1, 0, 1)
    for k in range(1, 8):
        a_copy(k).wait()
    for k in range(1, 4):
        x_copy(k).start()
    pair_loop(targets, moved, acc, 1, 10, 1, 5, 1)
    for y in range(4):
        sum_rows(acc, sums, 0, y)
        sum_rows(acc, sums, 5, y)
    for z in range(1, 5):
        sum_rows(acc, sums, z, 0)
        sum_rows(acc, sums, z, 3)
    for_sides(lambda n, s, c: back_copy(n, s, c).start())
    pair_loop(targets, moved, acc, 1, 3, 1, 1, 4)
    for k in range(1, 4):
        x_copy(k).wait()
    for_rows(lambda copy: copy.start(), True)
    densities_three(two, three, grouped, m2m, zc)
    for k in range(1, 4):
        z_copy(k).start()
    pair_loop(targets, moved, acc, 4, 7, 1, 1, 4)
    for z in range(1, 5):
        for y in range(1, 3):
            sum_rows(acc, sums, z, y)
    for_rows(lambda copy: copy.wait_recv(), False)
    for k in range(1, 4):
        z_copy(k).wait()

    stack_sources(two, three, stacked, slab, col)
    loads[4].wait()
    loads[5].wait()
    far[...] = jnp.transpose(translate(stacked, matrix, tail, first))

    for_senders(lambda n, s, c: back_copy(n, s, c).wait_recv())
    for z in range(4):
        for y in range(2):
            value = sums[z + 1, y + 1]
            zb = {0: 0, 3: 5}.get(z)
            yb = {0: 0, 1: 3}[y]
            value = value + back[z + 1, yb]
            if zb is not None:
                value = value + back[zb, y + 1] + back[zb, yb]
            row = (z * 2 + y) * 4
            for i in range(QT):
                lines[row : row + 4, i * W : (i + 1) * W] = value[4 * i : 4 * i + 4]
    for_rows(lambda copy: copy.wait_send(), True)
    for_sides(lambda n, s, c: target_copy(n, s, c).wait_send())
    for_sides(lambda n, s, c: back_copy(n, s, c).wait_send())


MESH = pl.DeviceIdType.MESH
VMEM = pl.BlockSpec(memory_space=pltpu.VMEM)


def scratch(*shape, dtype=F32):
    return pltpu.VMEM(shape, dtype)


def body(offsets, charges, check_to_equiv, m2m_matrix, m2l_matrix):
    dma = pltpu.SemaphoreType.DMA
    lines, far = pl.pallas_call(
        whole_kernel,
        name="whole",
        out_shape=(
            jax.ShapeDtypeStruct((32, W * QT), F32),
            jax.ShapeDtypeStruct((24, NS), F32),
        ),
        in_specs=[pl.BlockSpec(memory_space=pl.ANY)] * 5,
        out_specs=(VMEM, VMEM),
        scratch_shapes=[
            scratch(4, 3, 2, W * Q),
            scratch(4, 2, W * Q),
            scratch(NS, NS),
            scratch(NS, 8 * NS),
            scratch(6, 4, 16, W),
            scratch(6, 4, 16, W),
            scratch(6, 4, 16, 8, W),
            scratch(6, 4, 16, W),
            scratch(3, 8, 4, Q, W),
            scratch(W, 8 * W),
            scratch(W, W),
            scratch(W, 8 * W),
            scratch(P_SIZE, Q, W),
            scratch(P_SIZE, Q, W),
            scratch(P_SIZE, Q, W),
            scratch(2, 8 * W, W, dtype=BF16),
            scratch(32, W),
            scratch(16, W),
            scratch(4, 16, 48, W),
            scratch(2, 8, 40, W),
            scratch(64, 8 * W),
            scratch(24, (K_ALL + W - 1) // W * W),
            scratch(NS, TILES * W),
            scratch(NS, REST),
            dma((6,)),
            dma((8,)),
            dma((8,)),
            dma((8,)),
            dma((8,)),
            dma((2,)),
            dma((7,)),
            dma((7,)),
            dma((3,)),
            dma((3,)),
            dma((3,)),
            dma((3,)),
            dma((4,)),
            dma((4,)),
            dma((4,)),
            dma((4,)),
        ],
        compiler_params=pltpu.CompilerParams(
            vmem_limit_bytes=58 * 1024 * 1024, collective_id=0, has_side_effects=True
        ),
        cost_estimate=pl.CostEstimate(flops=400000000, bytes_accessed=16000000, transcendentals=0),
    )(jnp.swapaxes(offsets, 1, 2), charges, check_to_equiv, m2m_matrix, m2l_matrix)
    near_field, far2, far3 = pl.pallas_call(
        finish_kernel,
        name="finish",
        out_shape=(
            jax.ShapeDtypeStruct((4, 2, 4, W * QT), F32),
            jax.ShapeDtypeStruct((16, NS), F32),
            jax.ShapeDtypeStruct((2, NS), F32),
        ),
        in_specs=[VMEM, VMEM],
        out_specs=(VMEM, VMEM, VMEM),
    )(lines, far)
    return near_field, jnp.transpose(far2), jnp.transpose(far3)


def solution(mesh):
    in_specs = (P("slab", "col", None, None), P("slab", "col", None), P(), P(), P())
    out_specs = (P("slab", "col", None, None), P(None, ("slab", "col")), P(None, ("slab", "col")))
    return jax.shard_map(body, mesh=mesh, in_specs=in_specs, out_specs=out_specs, check_vma=False)
```

```python
import jax
import jax.numpy as jnp
from jax import lax
from jax.experimental import pallas as pl
from jax.experimental.pallas import tpu as pltpu
from jax.sharding import PartitionSpec as P

Q = 64
QT = 4
P_SIZE = 5
NS = 98
W = 128
SOFTEN = 0.0625
CHECK_SIDE = 1.45
F32 = jnp.float32
BF16 = jnp.bfloat16

COORD = [(float(g) / (P_SIZE - 1) - 0.5) * (2.0 * CHECK_SIDE) + 0.5 for g in range(P_SIZE)]
SURFACE = [
    (a, b, c)
    for a in range(P_SIZE)
    for b in range(P_SIZE)
    for c in range(P_SIZE)
    if min(a, b, c) == 0 or max(a, b, c) == P_SIZE - 1
]
OFFSETS = [
    (z, y, x)
    for z in range(-3, 4)
    for y in range(-3, 4)
    for x in range(-3, 4)
    if max(abs(z), abs(y), abs(x)) >= 2
]
K_ALL = len(OFFSETS) * NS
TILES = 140
CHUNK = 28 * W
LAST = K_ALL // W * W
REST = K_ALL - LAST


def split(x):
    high = x.astype(BF16)
    return high, (x - high.astype(F32)).astype(BF16)


def dot(a, b):
    return jnp.dot(a, b, preferred_element_type=F32)


def dot_t(a, b):
    return lax.dot_general(a, b, (((1,), (1,)), ((), ())), preferred_element_type=F32)


def dot3(a, b, d=dot):
    ah, al = split(a)
    bh, bl = split(b)
    return d(ah, bh) + d(ah, bl) + d(al, bh)


def squares_and_checks(src_ref, check, zz, yy, xx):
    def one_row(row, carry):
        for comp, table in ((0, zz), (1, yy), (2, xx)):
            value = src_ref[row, comp]
            for g in range(P_SIZE):
                delta = COORD[g] - value
                table[g] = delta * delta
        charge = src_ref[row, 3]
        lanes = pl.ds(pl.multiple_of(row * W, W), W)
        pair = None
        for k, (a, b, c) in enumerate(SURFACE):
            if pair != (a, b):
                pair, plane = (a, b), zz[a] + yy[b]
            term = charge * lax.rsqrt(plane + xx[c])
            check[k : k + 1, lanes] = jnp.sum(term, axis=0, keepdims=True)
        return carry

    lax.fori_loop(0, 8, one_row, 0)


def pad_matrices(c2e_ref, m2m_ref, c2e, m2m):
    c2e[...] = jnp.zeros_like(c2e)
    m2m[...] = jnp.zeros_like(m2m)
    c2e[0:NS, 0:NS] = c2e_ref[...]
    for octant in range(8):
        m2m[0:NS, octant * W : octant * W + NS] = m2m_ref[:, octant * NS : (octant + 1) * NS]


def upward_two(check, c2e, m2m, grouped, parity):
    density = dot3(c2e[...], check[...])
    high, low = split(density)
    leaf = lax.broadcasted_iota(jnp.int32, (2 * W, W), 0)
    lane = lax.broadcasted_iota(jnp.int32, (2 * W, W), 1)
    cell = (lane // 64) * W + 2 * (lane % 32) + (lane // 32) % 2
    for bx in range(2):
        pick = jnp.where(leaf == cell + 64 * bx, 1.0, 0.0).astype(BF16)
        for bz in range(2):
            for by in range(2):
                one, two = (bz * 2 + by) * W, ((bz + 2) * 2 + by) * W
                octant = 4 * bz + 2 * by + bx
                for half, part in enumerate((high, low)):
                    both = jnp.concatenate([part[:, one : one + W], part[:, two : two + W]], axis=1)
                    grouped[half, octant * W : (octant + 1) * W, :] = dot(both, pick).astype(BF16)
    mh, ml = split(m2m[...])
    level_one = dot(mh, grouped[0]) + dot(mh, grouped[1]) + dot(ml, grouped[0])
    turned = jnp.transpose(level_one)
    total = jnp.zeros((32, W), F32)
    for bz in range(2):
        for bx in range(2):
            at = pl.multiple_of((4 * bz + 2 * parity + bx) * W, W)
            block = turned[(bz * 2 + bx) * 32 : (bz * 2 + bx + 1) * 32]
            total = total + dot3(block, m2m[:, pl.ds(at, W)], dot_t)
    return total


def arrange_sources(positions, charge, moved, z):
    lane = lax.broadcasted_iota(jnp.int32, (Q, W), 1)

    def one(y, carry):
        row = 2 * z + y
        for comp in range(4):
            line = positions[z, comp, pl.ds(y, 1), :] if comp < 3 else charge[z, pl.ds(y, 1), :]
            turned = jnp.transpose(line.reshape(Q, W))
            value = jnp.concatenate([turned[0:Q], turned[Q : 2 * Q]], axis=1)
            half = pltpu.roll(value, 64, 1)
            left = jnp.where(lane < 64, pltpu.roll(value, 65, 1), half)
            right = jnp.where(lane < 64, half, pltpu.roll(value, 63, 1))
            if comp == 3:
                left = jnp.where(lane == 0, 0.0, left)
                right = jnp.where(lane == W - 1, 0.0, right)
            moved[0, row, comp] = left
            moved[1, row, comp] = value
            moved[2, row, comp] = right
        return carry

    lax.fori_loop(0, 2, one, 0)


def pair_rows(t_ref, moved, acc, zs, ys, sz, sy):
    tz, ty = zs + 1 - sz, ys + 1 - sy
    row = zs * 2 + ys
    centre = (sz == 0) & (sy == 0)
    sub = lax.broadcasted_iota(jnp.int32, (8, W), 0)
    rows = [jnp.broadcast_to(t_ref[tz, ty, k : k + 1, :], (8, W)) for k in range(12)]
    target_z = [rows[i] - sz.astype(F32) for i in range(QT)]
    target_y = [rows[QT + i] - sy.astype(F32) for i in range(QT)]
    sums = [jnp.zeros((8, W), F32) for _ in range(16)]
    for dx in range(3):
        target_x = [rows[2 * QT + i] - float(dx - 1) for i in range(QT)]
        for v in range(8):
            at = slice(8 * v, 8 * v + 8)
            z, y, x, q = [moved[dx, row, comp, at, :] for comp in range(4)]
            for i in range(QT):
                dz, dy, ddx = target_z[i] - z, target_y[i] - y, target_x[i] - x
                inverse = lax.rsqrt(dz * dz + dy * dy + (ddx * ddx + SOFTEN))
                weight = q * inverse
                if dx == 1 and v == 0:
                    weight = jnp.where((sub == i) & centre, 0.0, weight)
                cubed = weight * (inverse * inverse)
                sums[4 * i] += weight
                sums[4 * i + 1] += cubed * dz
                sums[4 * i + 2] += cubed * dy
                sums[4 * i + 3] += cubed * ddx
    for k in range(16):
        acc[tz, ty, k] += sums[k]


def pair_loop(t_ref, moved, acc, z_first, z_count, z_step, y_first, y_count, y_step=1):
    def one(p, carry):
        iz, iy = z_first + z_step * (p // y_count), y_first + y_step * (p % y_count)
        pair_rows(t_ref, moved, acc, iz // 3, iy // 3, 1 - iz % 3, 1 - iy % 3)
        return carry

    count = z_count * y_count
    lax.fori_loop(0, count, one, 0, unroll=4 if count % 4 == 0 else count // 2)


def sum_rows(acc, sums, z, y):
    sums[z, y] = jnp.sum(acc[z, y], axis=1)


def densities_three(two, three, grouped, m2m, zc):
    for n in range(4):
        z, y = n // 2, 2 * zc + n % 2
        for octant in range(8):
            bz, by, bx = octant // 4, octant // 2 % 2, octant % 2
            grouped[n * 16 : (n + 1) * 16, octant * W : (octant + 1) * W] = two[
                2 * z + bz, 2 * y + by, pl.ds(8 + bx, 16, stride=2), :
            ]
    level_three = dot3(grouped[...], m2m[...], dot_t)
    for n in range(4):
        three[n // 2, 2 * zc + n % 2, 8:24, :] = level_three[n * 16 : (n + 1) * 16]


def stack_sources(two, three, stacked, slab, col):
    z2, y2, x2 = slab, col // 2, 16 * (col % 2)
    z3, y3, x3 = slab // 2, 4 * (slab % 2) + col // 8, 2 * (col % 8)
    sub = lax.broadcasted_iota(jnp.int32, (24, W), 0)
    lane = lax.broadcasted_iota(jnp.int32, (24, W), 1)

    def use(cell, shift, size):
        at = cell + shift
        near = jnp.abs(at // 2 - cell // 2) <= 1
        return (at >= 0) & (at < size) & near, jnp.clip(at, 0, size - 1)

    for gz in range(-3, 4):
        chosen = [o for o, shift in enumerate(OFFSETS) if shift[0] == gz]

        @pl.when((slab + gz >= 0) & (slab + gz < 4))
        def _(chosen=chosen):
            pending = None
            for o in chosen:
                _, oy, ox = OFFSETS[o]
                oz = OFFSETS[o][0]
                uz2, sz2 = use(z2, oz, 4)
                uy2, sy2 = use(y2, oy, 16)
                uz3, sz3 = use(z3, oz, 2)
                uy3, sy3 = use(y3, oy, 8)
                keep2 = jnp.where(uz2 & uy2, 1.0, 0.0).astype(F32)
                keep3 = jnp.where(uz3 & uy3, 1.0, 0.0).astype(F32)
                value = jnp.concatenate(
                    [
                        two[sz2, sy2, pl.ds(8 + x2 + ox, 16), :] * keep2,
                        three[sz3, sy3, pl.ds(8 + x3 + ox, 8), :] * keep3,
                    ],
                    axis=0,
                )
                if ox == 3:
                    value = jnp.where(sub % 2 == 0, value, 0.0)
                if ox == -3:
                    value = jnp.where(sub % 2 == 1, value, 0.0)
                tile, start = divmod(o * NS, W)
                at = slice(tile * W, (tile + 1) * W)
                if start:
                    value = pltpu.roll(value, start, 1)
                    if pending is None:
                        pending = stacked[:, at]
                    filled = jnp.where(lane < start, pending, value)
                else:
                    filled = value
                if start + NS >= W:
                    stacked[:, at] = filled
                    pending = value if start + NS > W else None
                else:
                    pending = filled
            if pending is not None:
                tile, end = divmod((chosen[-1] + 1) * NS, W)
                stacked[:, tile * W : (tile + 1) * W] = jnp.where(lane < end, pending, 0.0)


def far_terms(matrix, sources):
    mh, ml = split(matrix)
    sh, sl = split(sources)
    return dot_t(mh, jnp.concatenate([sh, sl], axis=0)) + dot_t(ml, jnp.concatenate([sh, jnp.zeros_like(sl)], axis=0))


def translate(stacked, matrix, tail, first):
    def one(n, total):
        here = pl.ds(pl.multiple_of(n * CHUNK, W), CHUNK)
        there = pl.ds(pl.multiple_of(first + n * CHUNK, W), CHUNK)
        return total + far_terms(matrix[:, here], stacked[:, there])

    total = far_terms(tail[...], stacked[:, LAST:K_ALL])
    total = lax.fori_loop(0, TILES * W // CHUNK, one, total)
    return total[:, 0:24] + total[:, 24:48]


def finish_kernel(lines, far, out_ref, far2_ref, far3_ref):
    far2_ref[...] = far[0:16]
    far3_ref[...] = 0.5 * far[16:18]
    source = lax.broadcasted_iota(jnp.int32, (QT * W, QT * W), 0)
    place = lax.broadcasted_iota(jnp.int32, (QT * W, QT * W), 1)
    move = jnp.where(place == QT * (2 * (source % 64) + source // 64 % 2) + source // W, 1.0, 0.0).astype(BF16)
    value = lines[...]
    high, low = split(value)
    lowest = (value - high.astype(F32) - low.astype(F32)).astype(BF16)
    result = dot(high, move) + dot(low, move) + dot(lowest, move)
    for row in range(8):
        out_ref[row // 2, row % 2] = result[4 * row : 4 * row + 4]


SIDES = [(s, c) for s in (-1, 0, 1) for c in (-1, 0, 1) if (s, c) != (0, 0)]


def border(step, size):
    return {-1: slice(0, 1), 0: slice(1, size + 1), 1: slice(size + 1, size + 2)}[step]


def edge(step, size):
    return {-1: slice(1, 2), 0: slice(1, size + 1), 1: slice(size, size + 1)}[step]


def whole_kernel(
    positions_ref, charges_ref, c2e_ref, m2m_ref, m2l_ref, lines, far,
    positions, charge, c2e_in, m2m_in, targets, back, acc, sums, moved, m2m, c2e, check, zz, yy, xx, grouped_up,
    part, arrived, two, three, grouped, stacked, matrix, tail,
    load_sem, t_send, t_recv, b_send, b_recv, p_sem, a_send, a_recv, z_send, z_recv,
    up_send, up_recv, down_send, down_recv,
):
    slab, col = lax.axis_index("slab"), lax.axis_index("col")
    zc, xc, low_y = col // 8, (col // 2) % 4, col % 2
    place = slab * 2 + low_y

    def local_at(k):
        to = lax.rem(place + k % 8, 8)
        return to // 2, zc * 8 + lax.rem(xc + k // 8, 4) * 2 + lax.rem(to, 2)

    def along_z(k):
        return slab, lax.rem(zc + k, 4) * 8 + xc * 2 + low_y

    def exists(s, c):
        return (slab + s >= 0) & (slab + s < 4) & (col + c >= 0) & (col + c < 32)

    first = pl.multiple_of(W * (35 * (3 - slab) - jnp.where(slab == 0, 4, 0)), W)
    loads = [
        pltpu.make_async_copy(c2e_ref, c2e_in, load_sem.at[0]),
        pltpu.make_async_copy(m2m_ref, m2m_in, load_sem.at[1]),
        pltpu.make_async_copy(m2l_ref.at[:, pl.ds(first, TILES * W)], matrix, load_sem.at[2]),
        pltpu.make_async_copy(m2l_ref.at[:, pl.ds(LAST, REST)], tail, load_sem.at[3]),
    ]
    rows_in = [pltpu.make_async_copy(positions_ref.at[z], positions.at[z], load_sem.at[4 + z]) for z in range(4)]
    charges_in = [pltpu.make_async_copy(charges_ref.at[z], charge.at[z], load_sem.at[8 + z]) for z in range(4)]
    for z in range(4):
        rows_in[z].start()
        charges_in[z].start()
    for load in loads:
        load.start()

    targets[...] = jnp.zeros_like(targets)
    back[...] = jnp.zeros_like(back)
    three[...] = jnp.zeros_like(three)
    two[:, :, 0:8, :] = jnp.zeros((4, 16, 8, W), F32)
    two[:, :, 40:48, :] = jnp.zeros((4, 16, 8, W), F32)

    barrier = pltpu.get_barrier_semaphore()
    others = [local_at(k) for k in range(1, 32)]
    others += [along_z(k) for k in range(1, 4)]
    for other in others:
        pl.semaphore_signal(barrier, inc=1, device_id=other, device_id_type=MESH)
    outward = 2 * low_y - 1
    for s in (-1, 0, 1):
        @pl.when(exists(s, outward))
        def _(s=s):
            pl.semaphore_signal(barrier, inc=1, device_id=(slab + s, col + outward), device_id_type=MESH)

    acc[...] = jnp.zeros_like(acc)
    stacked[...] = jnp.zeros_like(stacked)
    check[NS:W, :] = jnp.zeros((W - NS, 8 * W), F32)
    for z in range(4):
        rows_in[z].wait()
        charges_in[z].wait()
        arrange_sources(positions, charge, moved, z)
    for row in range(8):
        for comp in range(3):
            targets[row // 2 + 1, row % 2 + 1, comp * QT : (comp + 1) * QT, :] = moved[1, row, comp, 0:QT, :]
    loads[0].wait()
    loads[1].wait()
    pad_matrices(c2e_in, m2m_in, c2e, m2m)

    more = sum(jnp.where(exists(s, outward), 1, 0) for s in (-1, 0, 1))
    pl.semaphore_wait(barrier, len(others) + more)

    def target_copy(n, s, c):
        return pltpu.make_async_remote_copy(
            src_ref=targets.at[edge(s, 4), edge(c, 2)],
            dst_ref=targets.at[border(-s, 4), border(-c, 2)],
            send_sem=t_send.at[n],
            recv_sem=t_recv.at[n],
            device_id=(slab + s, col + c),
            device_id_type=MESH,
        )

    def back_copy(n, s, c):
        return pltpu.make_async_remote_copy(
            src_ref=sums.at[border(s, 4), border(c, 2)],
            dst_ref=back.at[border(-s, 4), border(-c, 2)],
            send_sem=b_send.at[n],
            recv_sem=b_recv.at[n],
            device_id=(slab + s, col + c),
            device_id_type=MESH,
        )

    def for_sides(act):
        for n, (s, c) in enumerate(SIDES):
            @pl.when(exists(s, c))
            def _(n=n, s=s, c=c):
                act(n, s, c)

    def for_senders(act):
        for n, (s, c) in enumerate(SIDES):
            @pl.when(exists(-s, -c))
            def _(n=n, s=s, c=c):
                act(n, s, c)

    for_sides(lambda n, s, c: target_copy(n, s, c).start())

    squares_and_checks(moved.at[1], check, zz, yy, xx)
    part[...] = upward_two(check, c2e, m2m, grouped_up, low_y)
    theirs = pl.ds(pl.multiple_of(16 - 16 * low_y, 16), 16)
    pair_copy = pltpu.make_async_remote_copy(
        src_ref=part.at[theirs],
        dst_ref=arrived,
        send_sem=p_sem.at[0],
        recv_sem=p_sem.at[1],
        device_id=(slab, (col // 2) * 2 + 1 - low_y),
        device_id_type=MESH,
    )
    pair_copy.start()

    for_senders(lambda n, s, c: target_copy(n, s, c).wait_recv())
    pair_loop(targets, moved, acc, 0, 1, 1, 0, 6)

    pair_copy.wait()
    mine = pl.ds(pl.multiple_of(16 * low_y, 16), 16)
    here = pl.ds(pl.multiple_of(8 + 16 * low_y, 8), 16)
    two[slab, col // 2, here, :] = part[mine, :] + arrived[...]

    def a_copy(k):
        block = two.at[slab, col // 2, here]
        return pltpu.make_async_remote_copy(
            src_ref=block, dst_ref=block, send_sem=a_send.at[k - 1], recv_sem=a_recv.at[k - 1],
            device_id=local_at(k), device_id_type=MESH,
        )

    def z_copy(k):
        block = three.at[:, pl.ds(2 * zc, 2), 8:24]
        return pltpu.make_async_remote_copy(
            src_ref=block, dst_ref=block, send_sem=z_send.at[k - 1], recv_sem=z_recv.at[k - 1],
            device_id=along_z(k), device_id_type=MESH,
        )

    def row_copy(r, step):
        send, recv = (up_send, up_recv) if step == 1 else (down_send, down_recv)
        block = two.at[:, zc * 4 + r, 8:40]
        return pltpu.make_async_remote_copy(
            src_ref=block, dst_ref=block, send_sem=send.at[r], recv_sem=recv.at[r],
            device_id=(slab, col + 8 * step), device_id_type=MESH,
        )

    def for_rows(act, sender):
        for r in range(4):
            if r > 0:
                @pl.when((r > xc) & ((zc < 3) if sender else (zc > 0)))
                def _(r=r):
                    act(row_copy(r, 1))
            if r < 3:
                @pl.when((r < xc) & ((zc > 0) if sender else (zc < 3)))
                def _(r=r):
                    act(row_copy(r, -1))

    for k in range(1, 32):
        a_copy(k).start()
    pair_loop(targets, moved, acc, 11, 1, 1, 0, 6)
    pair_loop(targets, moved, acc, 1, 10, 1, 0, 1)
    pair_loop(targets, moved, acc, 1, 10, 1, 5, 1)
    for y in range(4):
        sum_rows(acc, sums, 0, y)
        sum_rows(acc, sums, 5, y)
    for z in range(1, 5):
        sum_rows(acc, sums, z, 0)
        sum_rows(acc, sums, z, 3)
    for_sides(lambda n, s, c: back_copy(n, s, c).start())
    for k in range(1, 32):
        a_copy(k).wait()
    for_rows(lambda copy: copy.start(), True)
    densities_three(two, three, grouped, m2m, zc)
    for k in range(1, 4):
        z_copy(k).start()
    pair_loop(targets, moved, acc, 1, 10, 1, 1, 4)
    for z in range(1, 5):
        for y in range(1, 3):
            sum_rows(acc, sums, z, y)
    for_rows(lambda copy: copy.wait_recv(), False)
    for k in range(1, 4):
        z_copy(k).wait()

    stack_sources(two, three, stacked, slab, col)
    loads[2].wait()
    loads[3].wait()
    far[...] = jnp.transpose(translate(stacked, matrix, tail, first))

    for_senders(lambda n, s, c: back_copy(n, s, c).wait_recv())
    for z in range(4):
        for y in range(2):
            value = sums[z + 1, y + 1]
            zb = {0: 0, 3: 5}.get(z)
            yb = {0: 0, 1: 3}[y]
            value = value + back[z + 1, yb]
            if zb is not None:
                value = value + back[zb, y + 1] + back[zb, yb]
            row = (z * 2 + y) * 4
            for i in range(QT):
                lines[row : row + 4, i * W : (i + 1) * W] = value[4 * i : 4 * i + 4]
    for_rows(lambda copy: copy.wait_send(), True)
    for_sides(lambda n, s, c: target_copy(n, s, c).wait_send())
    for_sides(lambda n, s, c: back_copy(n, s, c).wait_send())


MESH = pl.DeviceIdType.MESH
VMEM = pl.BlockSpec(memory_space=pltpu.VMEM)


def scratch(*shape, dtype=F32):
    return pltpu.VMEM(shape, dtype)


def body(offsets, charges, check_to_equiv, m2m_matrix, m2l_matrix):
    dma = pltpu.SemaphoreType.DMA
    lines, far = pl.pallas_call(
        whole_kernel,
        name="whole",
        out_shape=(
            jax.ShapeDtypeStruct((32, W * QT), F32),
            jax.ShapeDtypeStruct((24, NS), F32),
        ),
        in_specs=[pl.BlockSpec(memory_space=pl.ANY)] * 5,
        out_specs=(VMEM, VMEM),
        scratch_shapes=[
            scratch(4, 3, 2, W * Q),
            scratch(4, 2, W * Q),
            scratch(NS, NS),
            scratch(NS, 8 * NS),
            scratch(6, 4, 16, W),
            scratch(6, 4, 16, W),
            scratch(6, 4, 16, 8, W),
            scratch(6, 4, 16, W),
            scratch(3, 8, 4, Q, W),
            scratch(W, 8 * W),
            scratch(W, W),
            scratch(W, 8 * W),
            scratch(P_SIZE, Q, W),
            scratch(P_SIZE, Q, W),
            scratch(P_SIZE, Q, W),
            scratch(2, 8 * W, W, dtype=BF16),
            scratch(32, W),
            scratch(16, W),
            scratch(4, 16, 48, W),
            scratch(2, 8, 40, W),
            scratch(64, 8 * W),
            scratch(24, (K_ALL + W - 1) // W * W),
            scratch(NS, TILES * W),
            scratch(NS, REST),
            dma((12,)),
            dma((8,)),
            dma((8,)),
            dma((8,)),
            dma((8,)),
            dma((2,)),
            dma((31,)),
            dma((31,)),
            dma((3,)),
            dma((3,)),
            dma((4,)),
            dma((4,)),
            dma((4,)),
            dma((4,)),
        ],
        compiler_params=pltpu.CompilerParams(
            vmem_limit_bytes=58 * 1024 * 1024, collective_id=0, has_side_effects=True
        ),
        cost_estimate=pl.CostEstimate(flops=400000000, bytes_accessed=16000000, transcendentals=0),
    )(jnp.swapaxes(offsets, 1, 2), charges, check_to_equiv, m2m_matrix, m2l_matrix)
    near_field, far2, far3 = pl.pallas_call(
        finish_kernel,
        name="finish",
        out_shape=(
            jax.ShapeDtypeStruct((4, 2, 4, W * QT), F32),
            jax.ShapeDtypeStruct((16, NS), F32),
            jax.ShapeDtypeStruct((2, NS), F32),
        ),
        in_specs=[VMEM, VMEM],
        out_specs=(VMEM, VMEM, VMEM),
    )(lines, far)
    return near_field, jnp.transpose(far2), jnp.transpose(far3)


def solution(mesh):
    in_specs = (P("slab", "col", None, None), P("slab", "col", None), P(), P(), P())
    out_specs = (P("slab", "col", None, None), P(None, ("slab", "col")), P(None, ("slab", "col")))
    return jax.shard_map(body, mesh=mesh, in_specs=in_specs, out_specs=out_specs, check_vma=False)
```

```python
import jax
import jax.numpy as jnp
from jax import lax
from jax.experimental import pallas as pl
from jax.experimental.pallas import tpu as pltpu
from jax.sharding import PartitionSpec as P

Q = 64
QT = 4
P_SIZE = 5
NS = 98
W = 128
SOFTEN = 0.0625
CHECK_SIDE = 1.45
F32 = jnp.float32
BF16 = jnp.bfloat16

COORD = [(float(g) / (P_SIZE - 1) - 0.5) * (2.0 * CHECK_SIDE) + 0.5 for g in range(P_SIZE)]
SURFACE = [
    (a, b, c)
    for a in range(P_SIZE)
    for b in range(P_SIZE)
    for c in range(P_SIZE)
    if min(a, b, c) == 0 or max(a, b, c) == P_SIZE - 1
]
OFFSETS = [
    (z, y, x)
    for z in range(-3, 4)
    for y in range(-3, 4)
    for x in range(-3, 4)
    if max(abs(z), abs(y), abs(x)) >= 2
]
K_ALL = len(OFFSETS) * NS
TILES = 140
CHUNK = 28 * W
LAST = K_ALL // W * W
REST = K_ALL - LAST


def split(x):
    high = x.astype(BF16)
    return high, (x - high.astype(F32)).astype(BF16)


def dot(a, b):
    return jnp.dot(a, b, preferred_element_type=F32)


def dot_t(a, b):
    return lax.dot_general(a, b, (((1,), (1,)), ((), ())), preferred_element_type=F32)


def dot3(a, b, d=dot):
    ah, al = split(a)
    bh, bl = split(b)
    return d(ah, bh) + d(ah, bl) + d(al, bh)


def squares_and_checks(src_ref, check, zz, yy, xx):
    def one_row(row, carry):
        for comp, table in ((0, zz), (1, yy), (2, xx)):
            value = src_ref[row, comp]
            for g in range(P_SIZE):
                delta = COORD[g] - value
                table[g] = delta * delta
        charge = src_ref[row, 3]
        lanes = pl.ds(pl.multiple_of(row * W, W), W)
        pair = None
        for k, (a, b, c) in enumerate(SURFACE):
            if pair != (a, b):
                pair, plane = (a, b), zz[a] + yy[b]
            term = charge * lax.rsqrt(plane + xx[c])
            check[k : k + 1, lanes] = jnp.sum(term, axis=0, keepdims=True)
        return carry

    lax.fori_loop(0, 8, one_row, 0)


def pad_matrices(c2e_ref, m2m_ref, c2e, m2m):
    c2e[...] = jnp.zeros_like(c2e)
    m2m[...] = jnp.zeros_like(m2m)
    c2e[0:NS, 0:NS] = c2e_ref[...]
    for octant in range(8):
        m2m[0:NS, octant * W : octant * W + NS] = m2m_ref[:, octant * NS : (octant + 1) * NS]


def upward_two(check, c2e, m2m, grouped, parity):
    density = dot3(c2e[...], check[...])
    high, low = split(density)
    leaf = lax.broadcasted_iota(jnp.int32, (2 * W, W), 0)
    lane = lax.broadcasted_iota(jnp.int32, (2 * W, W), 1)
    cell = (lane // 64) * W + 2 * (lane % 32) + (lane // 32) % 2
    for bx in range(2):
        pick = jnp.where(leaf == cell + 64 * bx, 1.0, 0.0).astype(BF16)
        for bz in range(2):
            for by in range(2):
                one, two = (bz * 2 + by) * W, ((bz + 2) * 2 + by) * W
                octant = 4 * bz + 2 * by + bx
                for half, part in enumerate((high, low)):
                    both = jnp.concatenate([part[:, one : one + W], part[:, two : two + W]], axis=1)
                    grouped[half, octant * W : (octant + 1) * W, :] = dot(both, pick).astype(BF16)
    mh, ml = split(m2m[...])
    level_one = dot(mh, grouped[0]) + dot(mh, grouped[1]) + dot(ml, grouped[0])
    turned = jnp.transpose(level_one)
    total = jnp.zeros((32, W), F32)
    for bz in range(2):
        for bx in range(2):
            at = pl.multiple_of((4 * bz + 2 * parity + bx) * W, W)
            block = turned[(bz * 2 + bx) * 32 : (bz * 2 + bx + 1) * 32]
            total = total + dot3(block, m2m[:, pl.ds(at, W)], dot_t)
    return total


def arrange_sources(positions, charge, moved, z):
    lane = lax.broadcasted_iota(jnp.int32, (Q, W), 1)

    def one(y, carry):
        row = 2 * z + y
        for comp in range(4):
            line = positions[z, comp, pl.ds(y, 1), :] if comp < 3 else charge[z, pl.ds(y, 1), :]
            turned = jnp.transpose(line.reshape(Q, W))
            value = jnp.concatenate([turned[0:Q], turned[Q : 2 * Q]], axis=1)
            half = pltpu.roll(value, 64, 1)
            left = jnp.where(lane < 64, pltpu.roll(value, 65, 1), half)
            right = jnp.where(lane < 64, half, pltpu.roll(value, 63, 1))
            if comp == 3:
                left = jnp.where(lane == 0, 0.0, left)
                right = jnp.where(lane == W - 1, 0.0, right)
            moved[0, row, comp] = left
            moved[1, row, comp] = value
            moved[2, row, comp] = right
        return carry

    lax.fori_loop(0, 2, one, 0)


def pair_rows(t_ref, moved, acc, zs, ys, sz, sy):
    tz, ty = zs + 1 - sz, ys + 1 - sy
    row = zs * 2 + ys
    centre = (sz == 0) & (sy == 0)
    sub = lax.broadcasted_iota(jnp.int32, (8, W), 0)
    rows = [jnp.broadcast_to(t_ref[tz, ty, k : k + 1, :], (8, W)) for k in range(12)]
    target_z = [rows[i] - sz.astype(F32) for i in range(QT)]
    target_y = [rows[QT + i] - sy.astype(F32) for i in range(QT)]
    sums = [jnp.zeros((8, W), F32) for _ in range(16)]
    for dx in range(3):
        target_x = [rows[2 * QT + i] - float(dx - 1) for i in range(QT)]
        for v in range(8):
            at = slice(8 * v, 8 * v + 8)
            z, y, x, q = [moved[dx, row, comp, at, :] for comp in range(4)]
            for i in range(QT):
                dz, dy, ddx = target_z[i] - z, target_y[i] - y, target_x[i] - x
                inverse = lax.rsqrt(dz * dz + dy * dy + (ddx * ddx + SOFTEN))
                weight = q * inverse
                if dx == 1 and v == 0:
                    weight = jnp.where((sub == i) & centre, 0.0, weight)
                cubed = weight * (inverse * inverse)
                sums[4 * i] += weight
                sums[4 * i + 1] += cubed * dz
                sums[4 * i + 2] += cubed * dy
                sums[4 * i + 3] += cubed * ddx
    for k in range(16):
        acc[tz, ty, k] += sums[k]


def pair_loop(t_ref, moved, acc, z_first, z_count, z_step, y_first, y_count, y_step=1):
    def one(p, carry):
        iz, iy = z_first + z_step * (p // y_count), y_first + y_step * (p % y_count)
        pair_rows(t_ref, moved, acc, iz // 3, iy // 3, 1 - iz % 3, 1 - iy % 3)
        return carry

    count = z_count * y_count
    lax.fori_loop(0, count, one, 0, unroll=4 if count % 4 == 0 else count // 2)


def sum_rows(acc, sums, z, y):
    sums[z, y] = jnp.sum(acc[z, y], axis=1)


def densities_three(two, three, grouped, m2m, zc):
    for n in range(4):
        z, y = n // 2, 2 * zc + n % 2
        for octant in range(8):
            bz, by, bx = octant // 4, octant // 2 % 2, octant % 2
            grouped[n * 16 : (n + 1) * 16, octant * W : (octant + 1) * W] = two[
                2 * z + bz, 2 * y + by, pl.ds(8 + bx, 16, stride=2), :
            ]
    level_three = dot3(grouped[...], m2m[...], dot_t)
    for n in range(4):
        three[n // 2, 2 * zc + n % 2, 8:24, :] = level_three[n * 16 : (n + 1) * 16]


def stack_sources(two, three, stacked, slab, col):
    z2, y2, x2 = slab, col // 2, 16 * (col % 2)
    z3, y3, x3 = slab // 2, 4 * (slab % 2) + col // 8, 2 * (col % 8)
    sub = lax.broadcasted_iota(jnp.int32, (24, W), 0)
    lane = lax.broadcasted_iota(jnp.int32, (24, W), 1)

    def use(cell, shift, size):
        at = cell + shift
        near = jnp.abs(at // 2 - cell // 2) <= 1
        return (at >= 0) & (at < size) & near, jnp.clip(at, 0, size - 1)

    for gz in range(-3, 4):
        chosen = [o for o, shift in enumerate(OFFSETS) if shift[0] == gz]

        @pl.when((slab + gz >= 0) & (slab + gz < 4))
        def _(chosen=chosen):
            pending = None
            for o in chosen:
                _, oy, ox = OFFSETS[o]
                oz = OFFSETS[o][0]
                uz2, sz2 = use(z2, oz, 4)
                uy2, sy2 = use(y2, oy, 16)
                uz3, sz3 = use(z3, oz, 2)
                uy3, sy3 = use(y3, oy, 8)
                keep2 = jnp.where(uz2 & uy2, 1.0, 0.0).astype(F32)
                keep3 = jnp.where(uz3 & uy3, 1.0, 0.0).astype(F32)
                value = jnp.concatenate(
                    [
                        two[sz2, sy2, pl.ds(8 + x2 + ox, 16), :] * keep2,
                        three[sz3, sy3, pl.ds(8 + x3 + ox, 8), :] * keep3,
                    ],
                    axis=0,
                )
                if ox == 3:
                    value = jnp.where(sub % 2 == 0, value, 0.0)
                if ox == -3:
                    value = jnp.where(sub % 2 == 1, value, 0.0)
                tile, start = divmod(o * NS, W)
                at = slice(tile * W, (tile + 1) * W)
                if start:
                    value = pltpu.roll(value, start, 1)
                    if pending is None:
                        pending = stacked[:, at]
                    filled = jnp.where(lane < start, pending, value)
                else:
                    filled = value
                if start + NS >= W:
                    stacked[:, at] = filled
                    pending = value if start + NS > W else None
                else:
                    pending = filled
            if pending is not None:
                tile, end = divmod((chosen[-1] + 1) * NS, W)
                stacked[:, tile * W : (tile + 1) * W] = jnp.where(lane < end, pending, 0.0)


def far_terms(matrix, sources):
    mh, ml = split(matrix)
    sh, sl = split(sources)
    return dot_t(mh, jnp.concatenate([sh, sl], axis=0)) + dot_t(ml, jnp.concatenate([sh, jnp.zeros_like(sl)], axis=0))


def translate(stacked, matrix, tail, first):
    def one(n, total):
        here = pl.ds(pl.multiple_of(n * CHUNK, W), CHUNK)
        there = pl.ds(pl.multiple_of(first + n * CHUNK, W), CHUNK)
        return total + far_terms(matrix[:, here], stacked[:, there])

    total = far_terms(tail[...], stacked[:, LAST:K_ALL])
    total = lax.fori_loop(0, TILES * W // CHUNK, one, total)
    return total[:, 0:24] + total[:, 24:48]


def finish_kernel(lines, far, out_ref, far2_ref, far3_ref):
    far2_ref[...] = far[0:16]
    far3_ref[...] = 0.5 * far[16:18]
    source = lax.broadcasted_iota(jnp.int32, (QT * W, QT * W), 0)
    place = lax.broadcasted_iota(jnp.int32, (QT * W, QT * W), 1)
    move = jnp.where(place == QT * (2 * (source % 64) + source // 64 % 2) + source // W, 1.0, 0.0).astype(BF16)
    value = lines[...]
    high, low = split(value)
    lowest = (value - high.astype(F32) - low.astype(F32)).astype(BF16)
    result = dot(high, move) + dot(low, move) + dot(lowest, move)
    for row in range(8):
        out_ref[row // 2, row % 2] = result[4 * row : 4 * row + 4]


SIDES = [(s, c) for s in (-1, 0, 1) for c in (-1, 0, 1) if (s, c) != (0, 0)]


def border(step, size):
    return {-1: slice(0, 1), 0: slice(1, size + 1), 1: slice(size + 1, size + 2)}[step]


def edge(step, size):
    return {-1: slice(1, 2), 0: slice(1, size + 1), 1: slice(size, size + 1)}[step]


def whole_kernel(
    positions_ref, charges_ref, c2e_ref, m2m_ref, m2l_ref, lines, far,
    positions, charge, c2e_in, m2m_in, targets, back, acc, sums, moved, m2m, c2e, check, zz, yy, xx, grouped_up,
    part, arrived, two, three, grouped, stacked, matrix, tail,
    load_sem, t_send, t_recv, b_send, b_recv, p_sem, a_send, a_recv, z_send, z_recv,
    up_send, up_recv, down_send, down_recv,
):
    slab, col = lax.axis_index("slab"), lax.axis_index("col")
    zc, xc, low_y = col // 8, (col // 2) % 4, col % 2
    place = slab * 2 + low_y

    def local_at(k):
        to = lax.rem(place + k % 8, 8)
        return to // 2, zc * 8 + lax.rem(xc + k // 8, 4) * 2 + lax.rem(to, 2)

    def along_z(k):
        return slab, lax.rem(zc + k, 4) * 8 + xc * 2 + low_y

    def exists(s, c):
        return (slab + s >= 0) & (slab + s < 4) & (col + c >= 0) & (col + c < 32)

    first = pl.multiple_of(W * (35 * (3 - slab) - jnp.where(slab == 0, 4, 0)), W)
    loads = [
        pltpu.make_async_copy(c2e_ref, c2e_in, load_sem.at[0]),
        pltpu.make_async_copy(m2m_ref, m2m_in, load_sem.at[1]),
        pltpu.make_async_copy(m2l_ref.at[:, pl.ds(first, TILES * W)], matrix, load_sem.at[2]),
        pltpu.make_async_copy(m2l_ref.at[:, pl.ds(LAST, REST)], tail, load_sem.at[3]),
    ]
    rows_in = [pltpu.make_async_copy(positions_ref.at[z], positions.at[z], load_sem.at[4 + z]) for z in range(4)]
    charges_in = [pltpu.make_async_copy(charges_ref.at[z], charge.at[z], load_sem.at[8 + z]) for z in range(4)]
    for z in range(4):
        rows_in[z].start()
        charges_in[z].start()
    for load in loads:
        load.start()

    targets[...] = jnp.zeros_like(targets)
    back[...] = jnp.zeros_like(back)
    three[...] = jnp.zeros_like(three)
    two[:, :, 0:8, :] = jnp.zeros((4, 16, 8, W), F32)
    two[:, :, 40:48, :] = jnp.zeros((4, 16, 8, W), F32)

    barrier = pltpu.get_barrier_semaphore()
    others = [local_at(k) for k in range(1, 32)]
    others += [along_z(k) for k in range(1, 4)]
    for other in others:
        pl.semaphore_signal(barrier, inc=1, device_id=other, device_id_type=MESH)
    outward = 2 * low_y - 1
    for s in (-1, 0, 1):
        @pl.when(exists(s, outward))
        def _(s=s):
            pl.semaphore_signal(barrier, inc=1, device_id=(slab + s, col + outward), device_id_type=MESH)

    acc[...] = jnp.zeros_like(acc)
    stacked[...] = jnp.zeros_like(stacked)
    check[NS:W, :] = jnp.zeros((W - NS, 8 * W), F32)
    for z in range(4):
        rows_in[z].wait()
        charges_in[z].wait()
        arrange_sources(positions, charge, moved, z)
    for row in range(8):
        for comp in range(3):
            targets[row // 2 + 1, row % 2 + 1, comp * QT : (comp + 1) * QT, :] = moved[1, row, comp, 0:QT, :]
    loads[0].wait()
    loads[1].wait()
    pad_matrices(c2e_in, m2m_in, c2e, m2m)

    more = sum(jnp.where(exists(s, outward), 1, 0) for s in (-1, 0, 1))
    pl.semaphore_wait(barrier, len(others) + more)

    def target_copy(n, s, c):
        return pltpu.make_async_remote_copy(
            src_ref=targets.at[edge(s, 4), edge(c, 2)],
            dst_ref=targets.at[border(-s, 4), border(-c, 2)],
            send_sem=t_send.at[n],
            recv_sem=t_recv.at[n],
            device_id=(slab + s, col + c),
            device_id_type=MESH,
        )

    def back_copy(n, s, c):
        return pltpu.make_async_remote_copy(
            src_ref=sums.at[border(s, 4), border(c, 2)],
            dst_ref=back.at[border(-s, 4), border(-c, 2)],
            send_sem=b_send.at[n],
            recv_sem=b_recv.at[n],
            device_id=(slab + s, col + c),
            device_id_type=MESH,
        )

    def for_sides(act):
        for n, (s, c) in enumerate(SIDES):
            @pl.when(exists(s, c))
            def _(n=n, s=s, c=c):
                act(n, s, c)

    def for_senders(act):
        for n, (s, c) in enumerate(SIDES):
            @pl.when(exists(-s, -c))
            def _(n=n, s=s, c=c):
                act(n, s, c)

    for_sides(lambda n, s, c: target_copy(n, s, c).start())

    squares_and_checks(moved.at[1], check, zz, yy, xx)
    part[...] = upward_two(check, c2e, m2m, grouped_up, low_y)
    theirs = pl.ds(pl.multiple_of(16 - 16 * low_y, 16), 16)
    pair_copy = pltpu.make_async_remote_copy(
        src_ref=part.at[theirs],
        dst_ref=arrived,
        send_sem=p_sem.at[0],
        recv_sem=p_sem.at[1],
        device_id=(slab, (col // 2) * 2 + 1 - low_y),
        device_id_type=MESH,
    )
    pair_copy.start()

    for_senders(lambda n, s, c: target_copy(n, s, c).wait_recv())
    pair_loop(targets, moved, acc, 0, 1, 1, 0, 6)

    pair_copy.wait()
    mine = pl.ds(pl.multiple_of(16 * low_y, 16), 16)
    here = pl.ds(pl.multiple_of(8 + 16 * low_y, 8), 16)
    two[slab, col // 2, here, :] = part[mine, :] + arrived[...]

    def a_copy(k):
        block = two.at[slab, col // 2, here]
        return pltpu.make_async_remote_copy(
            src_ref=block, dst_ref=block, send_sem=a_send.at[k - 1], recv_sem=a_recv.at[k - 1],
            device_id=local_at(k), device_id_type=MESH,
        )

    def z_copy(k):
        block = three.at[:, pl.ds(2 * zc, 2), 8:24]
        return pltpu.make_async_remote_copy(
            src_ref=block, dst_ref=block, send_sem=z_send.at[k - 1], recv_sem=z_recv.at[k - 1],
            device_id=along_z(k), device_id_type=MESH,
        )

    def row_copy(r, step):
        send, recv = (up_send, up_recv) if step == 1 else (down_send, down_recv)
        block = two.at[:, zc * 4 + r, pl.ds(pl.multiple_of(8 + 8 * low_y, 8), 24)]
        return pltpu.make_async_remote_copy(
            src_ref=block, dst_ref=block, send_sem=send.at[r], recv_sem=recv.at[r],
            device_id=(slab, col + 8 * step), device_id_type=MESH,
        )

    def for_rows(act, sender):
        for r in range(4):
            if r > 0:
                @pl.when((r > xc) & ((zc < 3) if sender else (zc > 0)))
                def _(r=r):
                    act(row_copy(r, 1))
            if r < 3:
                @pl.when((r < xc) & ((zc > 0) if sender else (zc < 3)))
                def _(r=r):
                    act(row_copy(r, -1))

    for k in range(1, 32):
        a_copy(k).start()
    pair_loop(targets, moved, acc, 11, 1, 1, 0, 6)
    pair_loop(targets, moved, acc, 1, 10, 1, 0, 1)
    pair_loop(targets, moved, acc, 1, 10, 1, 5, 1)
    for y in range(4):
        sum_rows(acc, sums, 0, y)
        sum_rows(acc, sums, 5, y)
    for z in range(1, 5):
        sum_rows(acc, sums, z, 0)
        sum_rows(acc, sums, z, 3)
    for_sides(lambda n, s, c: back_copy(n, s, c).start())
    pair_loop(targets, moved, acc, 1, 2, 1, 1, 4)
    for k in range(1, 32):
        a_copy(k).wait()
    for_rows(lambda copy: copy.start(), True)
    densities_three(two, three, grouped, m2m, zc)
    for k in range(1, 4):
        z_copy(k).start()
    pair_loop(targets, moved, acc, 3, 8, 1, 1, 4)
    for z in range(1, 5):
        for y in range(1, 3):
            sum_rows(acc, sums, z, y)
    for_rows(lambda copy: copy.wait_recv(), False)
    for k in range(1, 4):
        z_copy(k).wait()

    stack_sources(two, three, stacked, slab, col)
    loads[2].wait()
    loads[3].wait()
    far[...] = jnp.transpose(translate(stacked, matrix, tail, first))

    for_senders(lambda n, s, c: back_copy(n, s, c).wait_recv())
    for z in range(4):
        for y in range(2):
            value = sums[z + 1, y + 1]
            zb = {0: 0, 3: 5}.get(z)
            yb = {0: 0, 1: 3}[y]
            value = value + back[z + 1, yb]
            if zb is not None:
                value = value + back[zb, y + 1] + back[zb, yb]
            row = (z * 2 + y) * 4
            for i in range(QT):
                lines[row : row + 4, i * W : (i + 1) * W] = value[4 * i : 4 * i + 4]
    for_rows(lambda copy: copy.wait_send(), True)
    for_sides(lambda n, s, c: target_copy(n, s, c).wait_send())
    for_sides(lambda n, s, c: back_copy(n, s, c).wait_send())


MESH = pl.DeviceIdType.MESH
VMEM = pl.BlockSpec(memory_space=pltpu.VMEM)


def scratch(*shape, dtype=F32):
    return pltpu.VMEM(shape, dtype)


def body(offsets, charges, check_to_equiv, m2m_matrix, m2l_matrix):
    dma = pltpu.SemaphoreType.DMA
    lines, far = pl.pallas_call(
        whole_kernel,
        name="whole",
        out_shape=(
            jax.ShapeDtypeStruct((32, W * QT), F32),
            jax.ShapeDtypeStruct((24, NS), F32),
        ),
        in_specs=[pl.BlockSpec(memory_space=pl.ANY)] * 5,
        out_specs=(VMEM, VMEM),
        scratch_shapes=[
            scratch(4, 3, 2, W * Q),
            scratch(4, 2, W * Q),
            scratch(NS, NS),
            scratch(NS, 8 * NS),
            scratch(6, 4, 16, W),
            scratch(6, 4, 16, W),
            scratch(6, 4, 16, 8, W),
            scratch(6, 4, 16, W),
            scratch(3, 8, 4, Q, W),
            scratch(W, 8 * W),
            scratch(W, W),
            scratch(W, 8 * W),
            scratch(P_SIZE, Q, W),
            scratch(P_SIZE, Q, W),
            scratch(P_SIZE, Q, W),
            scratch(2, 8 * W, W, dtype=BF16),
            scratch(32, W),
            scratch(16, W),
            scratch(4, 16, 48, W),
            scratch(2, 8, 40, W),
            scratch(64, 8 * W),
            scratch(24, (K_ALL + W - 1) // W * W),
            scratch(NS, TILES * W),
            scratch(NS, REST),
            dma((12,)),
            dma((8,)),
            dma((8,)),
            dma((8,)),
            dma((8,)),
            dma((2,)),
            dma((31,)),
            dma((31,)),
            dma((3,)),
            dma((3,)),
            dma((4,)),
            dma((4,)),
            dma((4,)),
            dma((4,)),
        ],
        compiler_params=pltpu.CompilerParams(
            vmem_limit_bytes=58 * 1024 * 1024, collective_id=0, has_side_effects=True
        ),
        cost_estimate=pl.CostEstimate(flops=400000000, bytes_accessed=16000000, transcendentals=0),
    )(jnp.swapaxes(offsets, 1, 2), charges, check_to_equiv, m2m_matrix, m2l_matrix)
    near_field, far2, far3 = pl.pallas_call(
        finish_kernel,
        name="finish",
        out_shape=(
            jax.ShapeDtypeStruct((4, 2, 4, W * QT), F32),
            jax.ShapeDtypeStruct((16, NS), F32),
            jax.ShapeDtypeStruct((2, NS), F32),
        ),
        in_specs=[VMEM, VMEM],
        out_specs=(VMEM, VMEM, VMEM),
    )(lines, far)
    return near_field, jnp.transpose(far2), jnp.transpose(far3)


def solution(mesh):
    in_specs = (P("slab", "col", None, None), P("slab", "col", None), P(), P(), P())
    out_specs = (P("slab", "col", None, None), P(None, ("slab", "col")), P(None, ("slab", "col")))
    return jax.shard_map(body, mesh=mesh, in_specs=in_specs, out_specs=out_specs, check_vma=False)
```
